128 devices in a mesh: occ: 32 (over y, x, z_hi), vir: 4 (over z_lo, core).
Axes of the slice: x: 4, y: 4, z: 4 (z_hi: 2, z_lo: 2; z = z_hi * 2 + z_lo), core: 2. Of those that a mesh axis runs over, the one named last changes fastest.
Arguments:
- factors: bfloat16 [32, 1024, 2048], P('occ', 'vir'), may hold values from -0.047851562 to 0.047851562
- occupied_energy: float32 [32], replicated, may hold values from -1.5 to -0.5
- virtual_energy: float32 [1024], replicated, may hold values from 0.2 to 3
Outputs:
- dens_vv: float32 [1024, 1024], P(('occ', 'vir'))
- dens_oo: float32 [32, 32], replicated
The draws below stay inside these ranges and needn't reach their ends.
All inputs are finite; a program needn't handle non-finite values.
Results may differ from the reference program's by a relative error of at most 0.0065.
Values may be sent and summed in bfloat16 or wider, within the bound.
A program may use at most 64 MiB of HBM per device.

```python
import jax
import jax.numpy as jnp
from jax import lax

ORB_DEV = 1
NVIR = 1024
NAUX = 2048
NBATCH = 32
N_OCC = 32


def strengthened(entries, stream_key, source, target, shards_of, factor):
    owner, partner = [(jnp.arange(entries.shape[axis_at]) // (entries.shape[axis_at] // shards_of)).reshape([-1 if axis == axis_at else 1 for axis in range(entries.ndim)]) for axis_at in (source, target)]
    chosen = jax.random.permutation(stream_key, shards_of)[partner]
    strong = (owner == chosen) | (owner == (partner + shards_of // 2) % shards_of)
    return jnp.where(strong, factor * entries, entries)


def block_scale(key, shape, shards, least, top_value):
    def one(position, blocks):
        draws = jax.random.uniform(jax.random.fold_in(jax.random.fold_in(key, 6), position), (blocks,), jnp.float32, least / len(shards), top_value / len(shards))
        return jnp.repeat(jnp.exp(draws), shape[position] // blocks).reshape((-1,) + (1,) * (len(shape) - position - 1))

    factor_of = one(*shards[0])
    for cut in shards[1:]:
        factor_of = factor_of * one(*cut)
    return factor_of


def heavy_noise(rng, dims, deviation, reach, pieces, heavy, held_as=jnp.bfloat16):
    result = deviation * jax.random.normal(rng, dims, jnp.float32)
    if pieces:
        result = result * block_scale(rng, dims, pieces, -0.22, 0.18)
    return jnp.clip(strengthened(result, jax.random.fold_in(rng, 3), *heavy), -reach, reach).astype(held_as)


def setup_inputs(seed: int = 0) -> dict:
    key_list = jax.random.split(jax.random.key(seed), 4)
    factors = heavy_noise(key_list[0], (NBATCH, NVIR, NAUX), 0.008, 0.047851562, ((0, 32), (1, 4)), (0, 1, 32, 2.75))
    occupied_energy = jnp.clip(jax.random.uniform(key_list[1], (NBATCH,), jnp.float32, -1.5, -0.5), -1.5, -0.5)
    virtual_energy = jnp.clip(jax.random.uniform(key_list[2], (NVIR,), jnp.float32, 0.2, 3.0), 0.2, 3.0)
    return dict(factors=factors, occupied_energy=occupied_energy, virtual_energy=virtual_energy)


def reference(factors, occupied_energy, virtual_energy):
    partners = N_OCC // 4
    offsets = jnp.arange(partners, dtype=jnp.int32)
    inner = jnp.arange(ORB_DEV, dtype=jnp.int32)
    columns = jnp.arange(NBATCH, dtype=jnp.int32)
    highest = lax.Precision.HIGHEST

    def per_orbital(carry, orbital):
        vv_total, oo_total = carry
        batch = (orbital // ORB_DEV).astype(jnp.int32)
        partner_ids = (((batch + offsets) % N_OCC)[:, None] * ORB_DEV + inner[None, :]).reshape(-1).astype(jnp.int32)
        left = jnp.take(factors, orbital, axis=0).astype(jnp.float32)
        right = jnp.take(factors, partner_ids, axis=0).astype(jnp.float32)
        integrals = jnp.einsum('ap,jbp->jab', left, right, precision=highest).astype(jnp.bfloat16)
        swapped = jnp.swapaxes(integrals, 1, 2)
        own_energy = jnp.take(occupied_energy, orbital)
        partner_energy = jnp.take(occupied_energy, partner_ids)
        denom = (own_energy + partner_energy[:, None, None]) - virtual_energy[None, :, None] - virtual_energy[None, None, :]
        amps = (integrals.astype(jnp.float32) / denom).astype(jnp.bfloat16)
        tilde = ((2.0 * integrals.astype(jnp.float32) - swapped.astype(jnp.float32)) / denom).astype(jnp.bfloat16)
        vv_term = jnp.einsum('jab,jac->bc', amps.astype(jnp.float32), tilde.astype(jnp.float32), precision=highest)
        gram = -jnp.einsum('jab,kab->jk', amps.astype(jnp.float32), tilde.astype(jnp.float32), precision=highest)
        onehot = (partner_ids[:, None] == columns[None, :]).astype(jnp.float32)
        placed = jnp.dot(onehot.T, jnp.dot(gram, onehot, precision=highest), precision=highest)
        return (vv_total + vv_term, oo_total + placed), None

    start = (jnp.zeros((NVIR, NVIR), jnp.float32), jnp.zeros((NBATCH, NBATCH), jnp.float32))
    (dens_vv, dens_oo), _ = lax.scan(per_orbital, start, jnp.arange(NBATCH, dtype=jnp.int32))
    return dens_vv, dens_oo
```

```python
import jax
import jax.numpy as jnp
from jax import lax
from jax.experimental import pallas as pl
from jax.experimental.pallas import tpu as pltpu
from jax.sharding import PartitionSpec as P

MESH = pl.DeviceIdType.MESH
F32 = jnp.float32
BF16 = jnp.bfloat16
NT = (((1,), (1,)), ((), ()))
Q = 256
NV = 1024
NP = 2048
S = 8


def device(y, x, z, core):
    return ((y * 4 + x) * 2 + z // 2, (z % 2) * 2 + core)


def kernel(
    native, occ_e, vir_row, vir_col, vv_out, oo_out,
    whole, part, blocks, recv_k, local_k, acc, gram_acc,
    send0, recv0, send_y, recv_y, send_x, recv_x, send_z, recv_z, keep, oo_send, oo_recv,
    a_send, a_recv, p_recv, y_send, x_send, f_send, k_send, k_recv, r_send, r_recv, g_send, g_recv,
):
    occ = lax.axis_index("occ")
    vir = lax.axis_index("vir")
    y = occ // 8
    x = (occ // 2) % 4
    h = occ % 2
    z = 2 * h + vir // 2
    core = vir % 2
    other = 1 - core
    orbital = 2 * (4 * y + x) + core

    barrier = pltpu.get_barrier_semaphore()
    peers = [device(y, x, z, other)]
    for d in (1, 2, 3):
        peers.append(device((y + d) % 4, x, z, core))
        peers.append(device(y, (x + d) % 4, z, core))
        peers.append(device(y, x, (z + d) % 4, core))
        peers.append(device(y, x, (z + d) % 4, other))
    for peer in peers:
        pl.semaphore_signal(barrier, inc=1, device_id=peer, device_id_type=MESH)
    pl.semaphore_wait(barrier, len(peers))

    def remote(src, dst, ssem, rsem, target):
        return pltpu.make_async_remote_copy(
            src_ref=src, dst_ref=dst, send_sem=ssem, recv_sem=rsem,
            device_id=target, device_id_type=MESH,
        )

    def arrived(ref, sem):
        pltpu.make_async_copy(ref, ref, sem).wait()

    def gather(d):
        return remote(native, whole.at[vir], a_send.at[d], a_recv.at[vir], device(y, x, (z + d) % 4, h))

    for d in (1, 3, 2):
        gather(d).start()

    @pl.when(core == h)
    def _():
        pltpu.make_async_copy(native, whole.at[vir], a_recv.at[vir]).start()

    @pl.when(core != h)
    def _():
        gather(0).start()

    home = whole.at[z]
    arrived(home, a_recv.at[z])
    pltpu.make_async_copy(home, part.at[core], p_recv.at[core]).start()
    shift_y = remote(home, part.at[8 + core], y_send, p_recv.at[8 + core], device((y + 3) % 4, x, z, core))
    shift_y.start()

    def along_x(l, src):
        return remote(
            src, part.at[2 * l + core], x_send.at[l - 1], p_recv.at[2 * l + core],
            device(y, (x + 4 - l) % 4, z, core),
        )

    def forward(slot, src, sem):
        return remote(src, part.at[slot], f_send.at[sem], p_recv.at[slot], device(y, x, z, other))

    for l in (1, 3, 2):

        @pl.when(x >= l)
        def _():
            along_x(l, home).start()

    @pl.when(core == 1)
    def _():
        forward(1, home, 0).start()

    above = part.at[8 + core]
    arrived(above, p_recv.at[8 + core])
    for l in (1, 3, 2):

        @pl.when(x < l)
        def _():
            along_x(l, above).start()

    @pl.when(core == 0)
    def _():
        forward(8, above, 0).start()

    acc[...] = jnp.zeros_like(acc)
    arrived(part.at[core], p_recv.at[core])
    for d in (1, 2, 3):
        arrived(whole.at[(z + d) % 4], a_recv.at[(z + d) % 4])

    def block_copy(t, d):
        return remote(
            blocks.at[t, d], recv_k.at[t, pl.ds(z * Q, Q)], k_send.at[t, d - 1], k_recv.at[t, d - 1],
            device(y, x, (z + d) % 4, core),
        )

    def integrals(t):
        def one(step, _):
            d = (step + 1) % 4
            w = (z + d) % 4
            tile = lax.dot_general(part[core + t], whole[w], NT, preferred_element_type=F32).astype(BF16)
            local_k[t, pl.ds(pl.multiple_of(w * Q, Q), Q), :] = tile.T

            @pl.when(d == 0)
            def _():
                recv_k[t, pl.ds(pl.multiple_of(z * Q, Q), Q), :] = tile

            @pl.when(d != 0)
            def _():
                blocks[t, d] = tile
                block_copy(t, d).start()

            return 0

        lax.fori_loop(0, 4, one, 0)

    def amplitudes(t):
        for d in (1, 2, 3):
            arrived(recv_k.at[t, pl.ds(pl.multiple_of(((z + 4 - d) % 4) * Q, Q), Q)], k_recv.at[t, d - 1])
        pair_e = occ_e[orbital] + occ_e[(orbital + t) % 32]
        top = pair_e - vir_row[:, pl.ds(pl.multiple_of(z * Q, Q), Q)]

        def one(b, _):
            rows = pl.ds(pl.multiple_of(b * 128, 128), 128)
            inverse = 1.0 / (top - vir_col[rows, :])
            k = recv_k[t, rows, :].astype(F32)
            swapped = local_k[t, rows, :].astype(F32)
            recv_k[t, rows, :] = (k * inverse).astype(BF16)
            local_k[t, rows, :] = ((2.0 * k - swapped) * inverse).astype(BF16)
            return 0

        lax.fori_loop(0, 8, one, 0)

        def product(b, _):
            rows = pl.ds(pl.multiple_of(b * Q, Q), Q)
            term = lax.dot_general(recv_k[t, rows, :], local_k[t], NT, preferred_element_type=F32)
            groups = pl.ds(b * 16, 16)
            acc[groups] = acc[groups] + term.reshape(16, 2, 8, NV)
            return 0

        lax.fori_loop(0, 4, product, 0)

    integrals(0)

    def advance(t, _):
        @pl.when(t % 2 == 1)
        def _():
            l = (t + 1) // 2

            @pl.when(t < 7)
            def _():
                own = part.at[2 * l + core]
                arrived(own, p_recv.at[2 * l + core])
                forward(2 * l + core, own, l).start()

            arrived(part.at[core + t], p_recv.at[core + t])

        integrals(t)
        amplitudes(t - 1)
        return 0

    lax.fori_loop(1, S, advance, 0)
    amplitudes(S - 1)

    def to_other(g, _):
        groups = pl.ds(g * 16, 16)
        send0[pl.ds(pl.multiple_of(g * 128, 128), 128), :] = acc[groups, other].reshape(128, NV).astype(BF16)
        return 0

    lax.fori_loop(0, 4, to_other, 0)
    swap = remote(send0, recv0, r_send.at[0], r_recv.at[0], device(y, x, z, other))
    swap.start()

    gram_acc[...] = jnp.zeros_like(gram_acc)

    def gram(g, _):
        rows = pl.ds(pl.multiple_of(g * 32, 32), 32)
        left = recv_k[:, rows, :].reshape(Q, Q)
        right = local_k[:, rows, :].reshape(Q, Q)
        gram_acc[...] += lax.dot_general(left, right, NT, preferred_element_type=F32)
        return 0

    lax.fori_loop(0, NV // 32, gram, 0)
    r = lax.broadcasted_iota(jnp.int32, (Q, Q), 0)
    c = lax.broadcasted_iota(jnp.int32, (Q, Q), 1)
    diagonal = jnp.where(r % 32 == c % 32, -gram_acc[...], 0.0)
    n = lax.broadcasted_iota(jnp.int32, (128, Q), 0)
    m = lax.broadcasted_iota(jnp.int32, (128, Q), 1)
    place = jnp.where(n == (orbital + m // 32) % 32, 1.0, 0.0).astype(F32)
    highest = lax.Precision.HIGHEST
    half = lax.dot_general(place, diagonal, (((1,), (0,)), ((), ())), precision=highest, preferred_element_type=F32)
    placed = lax.dot_general(half, place, NT, precision=highest, preferred_element_type=F32)
    oo_send[0] = placed[:32]

    def oo_copy(stage, d, index, target):
        return remote(oo_send.at[stage], oo_recv.at[index], g_send.at[index], g_recv.at[index], target)

    oo_swap = oo_copy(0, 1, 0, device(y, x, z, other))
    oo_swap.start()

    swap.wait_recv()
    stage_y = []
    for d in (1, 2, 3, 0):
        at = (y + d) % 4
        total = acc[pl.ds(at * 16, 16), core].reshape(128, NV)
        total = total + recv0[pl.ds(pl.multiple_of(at * 128, 128), 128), :].astype(F32)
        if d:
            send_y[d - 1] = total.astype(BF16)
            copy = remote(send_y.at[d - 1], recv_y.at[d - 1], r_send.at[d], r_recv.at[d], device(at, x, z, core))
            copy.start()
            stage_y.append(copy)
        else:
            keep[...] = total
    oo_swap.wait_recv()
    oo_send[1] = oo_send[0] + oo_recv[0]
    oo_y = [oo_copy(1, d, d, device((y + d) % 4, x, z, core)) for d in (1, 2, 3)]
    for copy in oo_y:
        copy.start()
    for copy in stage_y:
        copy.wait_recv()
    keep[...] = ((keep[...] + recv_y[0].astype(F32)) + recv_y[1].astype(F32)) + recv_y[2].astype(F32)

    stage_x = []
    for d in (1, 2, 3):
        at = (x + d) % 4
        send_x[d - 1] = keep[pl.ds(pl.multiple_of(at * 32, 32), 32), :].astype(BF16)
        copy = remote(send_x.at[d - 1], recv_x.at[d - 1], r_send.at[3 + d], r_recv.at[3 + d], device(y, at, z, core))
        copy.start()
        stage_x.append(copy)
    for copy in oo_y:
        copy.wait_recv()
    oo_send[2] = ((oo_send[1] + oo_recv[1]) + oo_recv[2]) + oo_recv[3]
    oo_x = [oo_copy(2, d, 3 + d, device(y, (x + d) % 4, z, core)) for d in (1, 2, 3)]
    for copy in oo_x:
        copy.start()
    for copy in stage_x:
        copy.wait_recv()
    mine = pl.ds(pl.multiple_of(x * 32, 32), 32)
    total = ((keep[mine, :] + recv_x[0].astype(F32)) + recv_x[1].astype(F32)) + recv_x[2].astype(F32)
    keep[pl.ds(0, 32), :] = total

    stage_z = []
    for d in (1, 2, 3):
        at = (z + d) % 4
        send_z[d - 1] = keep[pl.ds(pl.multiple_of(at * 8, 8), 8), :]
        copy = remote(send_z.at[d - 1], recv_z.at[d - 1], r_send.at[6 + d], r_recv.at[6 + d], device(y, x, at, core))
        copy.start()
        stage_z.append(copy)
    for copy in oo_x:
        copy.wait_recv()
    oo_send[3] = ((oo_send[2] + oo_recv[4]) + oo_recv[5]) + oo_recv[6]
    oo_z = [oo_copy(3, d, 6 + d, device(y, x, (z + d) % 4, core)) for d in (1, 2, 3)]
    for copy in oo_z:
        copy.start()
    for copy in stage_z:
        copy.wait_recv()
    mine = pl.ds(pl.multiple_of(z * 8, 8), 8)
    vv_out[...] = ((keep[mine, :] + recv_z[0]) + recv_z[1]) + recv_z[2]
    for copy in oo_z:
        copy.wait_recv()
    total = ((oo_send[3] + oo_recv[7]) + oo_recv[8]) + oo_recv[9]
    oo_out[...] = total[:, :32]

    for d in (1, 2, 3):
        gather(d).wait_send()

    @pl.when(core != h)
    def _():
        gather(0).wait_send()

    shift_y.wait_send()
    for l in (1, 2, 3):
        along_x(l, home).wait_send()
        forward(2 * l + core, part.at[2 * l + core], l).wait_send()
    forward(1, home, 0).wait_send()

    def drain(t, _):
        for d in (1, 2, 3):
            block_copy(t, d).wait_send()
        return 0

    lax.fori_loop(0, S, drain, 0)
    for copy in [swap, oo_swap] + stage_y + stage_x + stage_z + oo_y + oo_x + oo_z:
        copy.wait_send()


def on_device(factors, occupied_energy, virtual_energy):
    dma = pltpu.SemaphoreType.DMA
    vmem = pl.BlockSpec(memory_space=pltpu.VMEM)
    return pl.pallas_call(
        kernel,
        out_shape=(
            jax.ShapeDtypeStruct((8, NV), F32),
            jax.ShapeDtypeStruct((32, 32), F32),
        ),
        in_specs=[vmem, pl.BlockSpec(memory_space=pltpu.SMEM), vmem, vmem],
        out_specs=(vmem, vmem),
        scratch_shapes=[
            pltpu.VMEM((4, Q, NP), BF16),
            pltpu.VMEM((10, Q, NP), BF16),
            pltpu.VMEM((S, 4, Q, Q), BF16),
            pltpu.VMEM((S, NV, Q), BF16),
            pltpu.VMEM((S, NV, Q), BF16),
            pltpu.VMEM((64, 2, 8, NV), F32),
            pltpu.VMEM((Q, Q), F32),
            pltpu.VMEM((512, NV), BF16),
            pltpu.VMEM((512, NV), BF16),
            pltpu.VMEM((3, 128, NV), BF16),
            pltpu.VMEM((3, 128, NV), BF16),
            pltpu.VMEM((3, 32, NV), BF16),
            pltpu.VMEM((3, 32, NV), BF16),
            pltpu.VMEM((3, 8, NV), F32),
            pltpu.VMEM((3, 8, NV), F32),
            pltpu.VMEM((128, NV), F32),
            pltpu.VMEM((4, 32, 128), F32),
            pltpu.VMEM((10, 32, 128), F32),
            dma((4,)),
            dma((4,)),
            dma((10,)),
            dma,
            dma((3,)),
            dma((4,)),
            dma((S, 3)),
            dma((S, 3)),
            dma((10,)),
            dma((10,)),
            dma((10,)),
            dma((10,)),
        ],
        compiler_params=pltpu.CompilerParams(
            collective_id=0, has_side_effects=True, vmem_limit_bytes=56 * 1024 * 1024
        ),
        cost_estimate=pl.CostEstimate(
            flops=14 * 10**9, bytes_accessed=2 * 10**6, transcendentals=0
        ),
    )(factors[0], occupied_energy, virtual_energy[None, :], virtual_energy[:, None])


def solution(mesh):
    return jax.shard_map(
        on_device,
        mesh=mesh,
        in_specs=(P("occ", "vir", None), P(), P()),
        out_specs=(P(("occ", "vir"), None), P()),
        check_vma=False,
    )
```

```python
import jax
import jax.numpy as jnp
from jax import lax
from jax.experimental import pallas as pl
from jax.experimental.pallas import tpu as pltpu
from jax.sharding import PartitionSpec as P

MESH = pl.DeviceIdType.MESH
F32 = jnp.float32
BF16 = jnp.bfloat16
NT = (((1,), (1,)), ((), ()))
Q = 256
NV = 1024
NP = 2048
S = 8
CH = 4
ROWS = Q // CH
NEAR, FAR = (1, 3), (2,)
PARTS = ((0, 384), (384, 384), (768, 256))


def device(y, x, z, core):
    return ((y * 4 + x) * 2 + z // 2, (z % 2) * 2 + core)


def kernel(
    native, occ_e, vir_row, vir_col, vv_out, oo_out,
    whole, part, blocks, recv_k, local_k, acc, gram_acc,
    send0, recv0, send1, recv1, keep1, send2, recv2, keep2, send3, recv3, oo_send, oo_recv,
    h_send, h_recv, a_send, a_recv, p_recv, y_send, x_send, f_send, k_send, k_recv,
    c_send, c_recv, r_send, r_recv, g_send, g_recv,
):
    occ = lax.axis_index("occ")
    vir = lax.axis_index("vir")
    y = occ // 8
    x = (occ // 2) % 4
    h = occ % 2
    z = 2 * h + vir // 2
    core = vir % 2
    other = 1 - core
    orbital = 2 * (4 * y + x) + core

    def quarter(at):
        return 2 * (at % 2) + at // 2

    qz = quarter(z)
    here = device(y, x, z, other)

    barrier = pltpu.get_barrier_semaphore()
    peers = [here]
    for d in (1, 2, 3):
        peers.append(device((y + d) % 4, x, z, core))
        peers.append(device(y, (x + d) % 4, z, core))
        peers.append(device(y, x, (z + d) % 4, core))
        peers.append(device(y, x, (z + d) % 4, other))
    for peer in peers:
        pl.semaphore_signal(barrier, inc=1, device_id=peer, device_id_type=MESH)
    pl.semaphore_wait(barrier, len(peers))

    def remote(src, dst, ssem, rsem, target):
        return pltpu.make_async_remote_copy(
            src_ref=src, dst_ref=dst, send_sem=ssem, recv_sem=rsem,
            device_id=target, device_id_type=MESH,
        )

    def arrived(ref, sem):
        pltpu.make_async_copy(ref, ref, sem).wait()

    def piece(ref, ch):
        return ref.at[pl.ds(ch * ROWS, ROWS)]

    home = whole.at[qz]
    above = part.at[8 + core]

    def swap_home(ch):
        return remote(
            piece(native, ch), piece(whole.at[vir], ch), h_send.at[ch], h_recv.at[ch],
            device(y, x, (z + 2) % 4, other),
        )

    @pl.when(core == h)
    def _():
        for ch in range(CH):
            pltpu.make_async_copy(piece(native, ch), piece(home, ch), h_recv.at[ch]).start()

    @pl.when(core != h)
    def _():
        for ch in range(CH):
            swap_home(ch).start()

    def gather(d):
        return remote(native, whole.at[vir], a_send.at[d], a_recv.at[vir], device(y, x, (z + d) % 4, h))

    def shift_y(ch):
        return remote(
            piece(home, ch), piece(above, ch), y_send.at[ch], p_recv.at[8 + core, ch],
            device((y + 3) % 4, x, z, core),
        )

    def along_x(l, src, ch):
        return remote(
            piece(src, ch), piece(part.at[2 * l + core], ch), x_send.at[l, ch], p_recv.at[2 * l + core, ch],
            device(y, (x + 4 - l) % 4, z, core),
        )

    def forward(slot, src, sem):
        return remote(src, part.at[slot], f_send.at[sem], p_recv.at[slot, 0], here)

    for ch in range(CH):
        arrived(piece(home, ch), h_recv.at[ch])
        shift_y(ch).start()
        for l in NEAR:

            @pl.when(x >= l)
            def _():
                along_x(l, home, ch).start()

    @pl.when(core == 1)
    def _():
        forward(1, home, 0).start()

    @pl.when(core != h)
    def _():
        for ch in range(CH):
            swap_home(ch).wait_send()
        for d in (0, 1, 3):
            gather(d).start()

    @pl.when(core == h)
    def _():
        arrived(whole.at[2 * (z % 2) + other], a_recv.at[2 * (z % 2) + other])
        for d in (1, 3, 2):
            gather(d).start()

    for ch in range(CH):
        arrived(piece(above, ch), p_recv.at[8 + core, ch])
        for l in NEAR:

            @pl.when(x < l)
            def _():
                along_x(l, above, ch).start()

    @pl.when(core == 0)
    def _():
        forward(8, above, 0).start()

    acc[...] = jnp.zeros_like(acc)
    for d in (1, 2, 3):
        q = quarter((z + d) % 4)

        @pl.when(jnp.logical_or(core != h, q != 2 * (z % 2) + other))
        def _():
            arrived(whole.at[q], a_recv.at[q])

    def block_copy(s, d):
        return remote(
            blocks.at[s, d], recv_k.at[s, pl.ds(qz * Q, Q)], k_send.at[s, d - 1], k_recv.at[s, d - 1],
            device(y, x, (z + d) % 4, core),
        )

    def integrals(s, source):
        def one(step, _):
            d = (step + 1) % 4
            w = quarter((z + d) % 4)
            tile = lax.dot_general(source[...], whole[w], NT, preferred_element_type=F32).astype(BF16)
            local_k[s, pl.ds(pl.multiple_of(w * Q, Q), Q), :] = tile.T

            @pl.when(d == 0)
            def _():
                recv_k[s, pl.ds(pl.multiple_of(qz * Q, Q), Q), :] = tile

            @pl.when(d != 0)
            def _():
                blocks[s, d] = tile
                block_copy(s, d).start()

            return 0

        lax.fori_loop(0, 4, one, 0)

    def amplitudes(s):
        for d in (1, 2, 3):
            q = quarter((z + 4 - d) % 4)
            arrived(recv_k.at[s, pl.ds(pl.multiple_of(q * Q, Q), Q)], k_recv.at[s, d - 1])
        pair_e = occ_e[orbital] + occ_e[(orbital + s) % 32]
        top = pair_e - vir_row[:, pl.ds(pl.multiple_of(qz * Q, Q), Q)]

        def one(b, _):
            rows = pl.ds(pl.multiple_of(b * 128, 128), 128)
            inverse = 1.0 / (top - vir_col[rows, :])
            k = recv_k[s, rows, :].astype(F32)
            swapped = local_k[s, rows, :].astype(F32)
            recv_k[s, rows, :] = (k * inverse).astype(BF16)
            local_k[s, rows, :] = ((2.0 * k - swapped) * inverse).astype(BF16)
            return 0

        lax.fori_loop(0, 8, one, 0)

        def product(b, _):
            rows = pl.ds(pl.multiple_of(b * Q, Q), Q)
            term = lax.dot_general(recv_k[s, rows, :], local_k[s], NT, preferred_element_type=F32)
            acc[b] = acc[b] + term.reshape(4, 4, 2, 8, NV)
            return 0

        lax.fori_loop(0, 4, product, 0)

    def slot_of(n):
        m = n + core
        return m + jnp.where((m == 4) | (m == 5), 2, 0) - jnp.where((m == 6) | (m == 7), 2, 0)

    integrals(0, home)
    for l in FAR:
        for k in NEAR:
            for ch in range(CH):
                along_x(k, home, ch).wait_send()

        @pl.when(x >= l)
        def _():
            for ch in range(CH):
                along_x(l, home, ch).start()

        @pl.when(x < l)
        def _():
            for ch in range(CH):
                along_x(l, above, ch).start()

    def advance(n, _):
        slot = slot_of(n)

        @pl.when(n % 2 == 1)
        def _():
            @pl.when(n < 7)
            def _():
                l = 1 + jnp.where(n == 3, 2, 0) + jnp.where(n == 5, 1, 0)
                mine = 2 * l + core
                for ch in range(CH):
                    arrived(piece(part.at[mine], ch), p_recv.at[mine, ch])
                forward(mine, part.at[mine], l).start()

            arrived(part.at[slot], p_recv.at[slot, 0])

        integrals(slot - core, part.at[slot])
        amplitudes(jnp.where(n == 1, 0, slot_of(n - 1) - core))
        return 0

    lax.fori_loop(1, S, advance, 0)
    amplitudes(slot_of(S - 1) - core)

    def to_other(g, _):
        rows = pl.ds(pl.multiple_of(g * 128, 128), 128)
        send0[rows, :] = acc[g, :, :, other].reshape(128, NV).astype(BF16)
        return 0

    lax.fori_loop(0, 4, to_other, 0)
    swap = remote(send0, recv0, c_send, c_recv, here)
    swap.start()

    gram_acc[...] = jnp.zeros_like(gram_acc)

    def gram(g, _):
        rows = pl.ds(pl.multiple_of(g * 32, 32), 32)
        left = recv_k[:, rows, :].reshape(Q, Q)
        right = local_k[:, rows, :].reshape(Q, Q)
        gram_acc[...] += lax.dot_general(left, right, NT, preferred_element_type=F32)
        return 0

    lax.fori_loop(0, NV // 32, gram, 0)
    r = lax.broadcasted_iota(jnp.int32, (Q, Q), 0)
    c = lax.broadcasted_iota(jnp.int32, (Q, Q), 1)
    diagonal = jnp.where(r % 32 == c % 32, -gram_acc[...], 0.0)
    n = lax.broadcasted_iota(jnp.int32, (128, Q), 0)
    m = lax.broadcasted_iota(jnp.int32, (128, Q), 1)
    place = jnp.where(n == (orbital + m // 32) % 32, 1.0, 0.0).astype(F32)
    highest = lax.Precision.HIGHEST
    half = lax.dot_general(place, diagonal, (((1,), (0,)), ((), ())), precision=highest, preferred_element_type=F32)
    placed = lax.dot_general(half, place, NT, precision=highest, preferred_element_type=F32)
    oo_send[0] = placed[:32]

    def oo_copy(stage, index, target):
        return remote(oo_send.at[stage], oo_recv.at[index], g_send.at[index], g_recv.at[index], target)

    oo_swap = oo_copy(0, 0, here)
    oo_swap.start()
    started = [swap, oo_swap]

    swap.wait_recv()

    def add_other(g, _):
        rows = pl.ds(pl.multiple_of(g * 128, 128), 128)
        acc[g, :, :, core] = acc[g, :, :, core] + recv0[rows, :].astype(F32).reshape(4, 4, 8, NV)
        return 0

    lax.fori_loop(0, 4, add_other, 0)

    def neighbour(axis, d):
        if axis == "y":
            return device((y + d) % 4, x, z, core), (y + d) % 4
        if axis == "x":
            return device(y, (x + d) % 4, z, core), (x + d) % 4
        return device(y, x, (z + d) % 4, core), (z + d) % 4

    def first(axis, at, cols):
        if axis == "y":
            return acc[at, :, :, core, :, cols]
        if axis == "x":
            return acc[:, at, :, core, :, cols]
        return acc[:, :, at, core, :, cols]

    def exchange(stage, send, recv, take, dtype, rows, axes):
        copies = []
        for d in (1, 2, 3):
            for p, (start, width) in enumerate(PARTS):
                target, at = neighbour(axes[p], d)
                cols = pl.ds(start, width)
                send[d - 1, :, cols] = take(p, at, cols).reshape(rows, width).astype(dtype)
                sem = 9 * stage + 3 * (d - 1) + p
                copy = remote(
                    send.at[d - 1, :, cols], recv.at[d - 1, :, cols], r_send.at[sem], r_recv.at[sem], target
                )
                copy.start()
                copies.append(copy)
        started.extend(copies)
        return copies

    def total(p, take, recv, axis, cols, shape):
        _, at = neighbour(axis, 0)
        value = take(p, at, cols)
        for d in (0, 1, 2):
            value = value + recv[d, :, cols].astype(F32).reshape(shape)
        return value

    def sum_oo(stage, low, high):
        value = oo_send[stage]
        for index in range(low, high):
            value = value + oo_recv[index]
        return value

    def oo_round(stage, low, axis):
        copies = [oo_copy(stage, low + d - 1, neighbour(axis, d)[0]) for d in (1, 2, 3)]
        for copy in copies:
            copy.start()
        started.extend(copies)
        return copies

    axes1, axes2, axes3 = ("y", "x", "z"), ("x", "z", "y"), ("z", "y", "x")

    def take1(p, at, cols):
        return first(axes1[p], at, cols)

    def take2(p, at, cols):
        return keep1[:, at, :, cols] if p == 1 else keep1[at, :, :, cols]

    def take3(p, at, cols):
        return keep2[at, :, cols]

    round1 = exchange(0, send1, recv1, take1, BF16, 128, axes1)
    oo_swap.wait_recv()
    oo_send[1] = sum_oo(0, 0, 1)
    oo1 = oo_round(1, 1, "y")
    for copy in round1:
        copy.wait_recv()
    for p, (start, width) in enumerate(PARTS):
        cols = pl.ds(start, width)
        keep1[:, :, :, cols] = total(p, take1, recv1, axes1[p], cols, (4, 4, 8, width))

    round2 = exchange(1, send2, recv2, take2, BF16, 32, axes2)
    for copy in oo1:
        copy.wait_recv()
    oo_send[2] = sum_oo(1, 1, 4)
    oo2 = oo_round(2, 4, "x")
    for copy in round2:
        copy.wait_recv()
    for p, (start, width) in enumerate(PARTS):
        cols = pl.ds(start, width)
        keep2[:, :, cols] = total(p, take2, recv2, axes2[p], cols, (4, 8, width))

    round3 = exchange(2, send3, recv3, take3, F32, 8, axes3)
    for copy in oo2:
        copy.wait_recv()
    oo_send[3] = sum_oo(2, 4, 7)
    oo3 = oo_round(3, 7, "z")
    for copy in round3:
        copy.wait_recv()
    for p, (start, width) in enumerate(PARTS):
        cols = pl.ds(start, width)
        vv_out[:, cols] = total(p, take3, recv3, axes3[p], cols, (8, width))
    for copy in oo3:
        copy.wait_recv()
    oo_out[...] = sum_oo(3, 7, 10)[:, :32]

    gather(1).wait_send()
    gather(3).wait_send()

    @pl.when(core == h)
    def _():
        gather(2).wait_send()

    @pl.when(core != h)
    def _():
        gather(0).wait_send()

    for ch in range(CH):
        shift_y(ch).wait_send()
        for l in FAR if FAR else NEAR:
            along_x(l, home, ch).wait_send()
    for l in (1, 2, 3):
        forward(2 * l + core, part.at[2 * l + core], l).wait_send()
    forward(1, home, 0).wait_send()

    def drain(s, _):
        for d in (1, 2, 3):
            block_copy(s, d).wait_send()
        return 0

    lax.fori_loop(0, S, drain, 0)
    for copy in started:
        copy.wait_send()


def on_device(factors, occupied_energy, virtual_energy):
    dma = pltpu.SemaphoreType.DMA
    vmem = pl.BlockSpec(memory_space=pltpu.VMEM)
    return pl.pallas_call(
        kernel,
        out_shape=(
            jax.ShapeDtypeStruct((8, NV), F32),
            jax.ShapeDtypeStruct((32, 32), F32),
        ),
        in_specs=[vmem, pl.BlockSpec(memory_space=pltpu.SMEM), vmem, vmem],
        out_specs=(vmem, vmem),
        scratch_shapes=[
            pltpu.VMEM((4, Q, NP), BF16),
            pltpu.VMEM((10, Q, NP), BF16),
            pltpu.VMEM((S, 4, Q, Q), BF16),
            pltpu.VMEM((S, NV, Q), BF16),
            pltpu.VMEM((S, NV, Q), BF16),
            pltpu.VMEM((4, 4, 4, 2, 8, NV), F32),
            pltpu.VMEM((Q, Q), F32),
            pltpu.VMEM((512, NV), BF16),
            pltpu.VMEM((512, NV), BF16),
            pltpu.VMEM((3, 128, NV), BF16),
            pltpu.VMEM((3, 128, NV), BF16),
            pltpu.VMEM((4, 4, 8, NV), F32),
            pltpu.VMEM((3, 32, NV), BF16),
            pltpu.VMEM((3, 32, NV), BF16),
            pltpu.VMEM((4, 8, NV), F32),
            pltpu.VMEM((3, 8, NV), F32),
            pltpu.VMEM((3, 8, NV), F32),
            pltpu.VMEM((4, 32, 128), F32),
            pltpu.VMEM((10, 32, 128), F32),
            dma((CH,)),
            dma((CH,)),
            dma((4,)),
            dma((4,)),
            dma((10, CH)),
            dma((CH,)),
            dma((4, CH)),
            dma((4,)),
            dma((S, 3)),
            dma((S, 3)),
            dma,
            dma,
            dma((27,)),
            dma((27,)),
            dma((10,)),
            dma((10,)),
        ],
        compiler_params=pltpu.CompilerParams(
            collective_id=0, has_side_effects=True, vmem_limit_bytes=56 * 1024 * 1024
        ),
        cost_estimate=pl.CostEstimate(
            flops=14 * 10**9, bytes_accessed=2 * 10**6, transcendentals=0
        ),
    )(factors[0], occupied_energy, virtual_energy[None, :], virtual_energy[:, None])


def solution(mesh):
    return jax.shard_map(
        on_device,
        mesh=mesh,
        in_specs=(P("occ", "vir", None), P(), P()),
        out_specs=(P(("occ", "vir"), None), P()),
        check_vma=False,
    )
```

```python
import jax
import jax.numpy as jnp
from jax import lax
from jax.experimental import pallas as pl
from jax.experimental.pallas import tpu as pltpu
from jax.sharding import PartitionSpec as P

MESH = pl.DeviceIdType.MESH
F32 = jnp.float32
BF16 = jnp.bfloat16
NT = (((1,), (1,)), ((), ()))
Q = 256
NV = 1024
NP = 2048
S = 8
CH = 4
ROWS = Q // CH
NEAR, FAR = (1, 3), (2,)
PARTS = ((0, 384), (384, 384), (768, 256))


def device(y, x, z, core):
    return ((y * 4 + x) * 2 + z // 2, (z % 2) * 2 + core)


def kernel(
    native, occ_e, vir_row, vir_col, vv_out, oo_out,
    whole, part, blocks, recv_k, local_k, acc, gram_acc,
    send0, recv0, send1, recv1, keep1, send2, recv2, keep2, send3, recv3, oo_send, oo_recv,
    h_send, h_recv, a_send, a_recv, p_recv, y_send, x_send, f_send, k_send, k_recv,
    b_send, b_recv, c_send, c_recv, r_send, r_recv, g_send, g_recv,
):
    occ = lax.axis_index("occ")
    vir = lax.axis_index("vir")
    y = occ // 8
    x = (occ // 2) % 4
    h = occ % 2
    z = 2 * h + vir // 2
    core = vir % 2
    other = 1 - core
    orbital = 2 * (4 * y + x) + core

    def quarter(at):
        return 2 * (at % 2) + at // 2

    qz = quarter(z)
    here = device(y, x, z, other)

    barrier = pltpu.get_barrier_semaphore()
    peers = [here]
    for d in (1, 2, 3):
        peers.append(device((y + d) % 4, x, z, core))
        peers.append(device((y + d) % 4, x, z, other))
        peers.append(device(y, x, (z + d) % 4, core))
        peers.append(device(y, x, (z + d) % 4, other))
        for e in range(4):
            peers.append(device(y, (x + d) % 4, (z + e) % 4, core))
    for peer in peers:
        pl.semaphore_signal(barrier, inc=1, device_id=peer, device_id_type=MESH)
    pl.semaphore_wait(barrier, len(peers))

    def remote(src, dst, ssem, rsem, target):
        return pltpu.make_async_remote_copy(
            src_ref=src, dst_ref=dst, send_sem=ssem, recv_sem=rsem,
            device_id=target, device_id_type=MESH,
        )

    def arrived(ref, sem):
        pltpu.make_async_copy(ref, ref, sem).wait()

    def piece(ref, ch):
        return ref.at[pl.ds(ch * ROWS, ROWS)]

    home = whole.at[qz]
    above = part.at[8 + core]

    def swap_home(ch):
        return remote(
            piece(native, ch), piece(whole.at[vir], ch), h_send.at[ch], h_recv.at[ch],
            device(y, x, (z + 2) % 4, other),
        )

    @pl.when(core == h)
    def _():
        for ch in range(CH):
            pltpu.make_async_copy(piece(native, ch), piece(home, ch), h_recv.at[ch]).start()

    @pl.when(core != h)
    def _():
        for ch in range(CH):
            swap_home(ch).start()

    def gather(d):
        return remote(native, whole.at[vir], a_send.at[d], a_recv.at[vir], device(y, x, (z + d) % 4, h))

    def shift_y(ch):
        return remote(
            piece(home, ch), piece(above, ch), y_send.at[ch], p_recv.at[8 + core, ch],
            device((y + 3) % 4, x, z, core),
        )

    def along_x(l, src, ch):
        return remote(
            piece(src, ch), piece(part.at[2 * l + core], ch), x_send.at[l, ch], p_recv.at[2 * l + core, ch],
            device(y, (x + 4 - l) % 4, z, core),
        )

    def forward(slot, src, sem):
        return remote(src, part.at[slot], f_send.at[sem], p_recv.at[slot, 0], here)

    for ch in range(CH):
        arrived(piece(home, ch), h_recv.at[ch])
        shift_y(ch).start()
        for l in NEAR:

            @pl.when(x >= l)
            def _():
                along_x(l, home, ch).start()

    @pl.when(core == 1)
    def _():
        forward(1, home, 0).start()

    @pl.when(core != h)
    def _():
        for d in (1, 3, 0):
            gather(d).start()

    for ch in range(CH):
        arrived(piece(above, ch), p_recv.at[8 + core, ch])
        for l in NEAR:

            @pl.when(x < l)
            def _():
                along_x(l, above, ch).start()

    @pl.when(core == h)
    def _():
        for d in (1, 3):
            gather(d).start()

    for l in FAR:

        @pl.when(x >= l)
        def _():
            for ch in range(CH):
                along_x(l, home, ch).start()

        @pl.when(x < l)
        def _():
            for ch in range(CH):
                along_x(l, above, ch).start()

    @pl.when(core == 0)
    def _():
        forward(8, above, 0).start()

    acc[...] = jnp.zeros_like(acc)
    place_z = (z + 4 - 2 * core) % 4
    plus = jnp.logical_and(place_z > 0, place_z < 3)
    passed = core + jnp.where(place_z % 2 == 0, 2, 0)
    distant = core + jnp.where(place_z == 3, 2, 0)

    def half_of(ref, part_index):
        return ref.at[pl.ds(pl.multiple_of(part_index * (Q // 2), Q // 2), Q // 2)]

    def pass_on():
        at = jnp.where(plus, 0, 1)
        return remote(
            half_of(whole.at[passed], at), half_of(whole.at[passed], at), b_send, b_recv.at[at],
            device(y, x, jnp.where(plus, z + 1, z + 3) % 4, core),
        )

    arrived(whole.at[passed], a_recv.at[passed])
    pass_on().start()

    @pl.when(place_z != 2)
    def _():
        arrived(whole.at[other], a_recv.at[other])

    @pl.when(place_z != 3)
    def _():
        arrived(whole.at[2 + other], a_recv.at[2 + other])

    @pl.when(place_z >= 2)
    def _():
        for part_index in (0, 1):
            arrived(half_of(whole.at[distant], part_index), b_recv.at[part_index])

    def block_copy(s, w):
        return remote(
            blocks.at[s, w], recv_k.at[s, pl.ds(qz * Q, Q)], k_send.at[s, w], k_recv.at[s, qz],
            device(y, x, quarter(w), core),
        )

    def integrals(s, source):
        for w in range(4):
            tile = lax.dot_general(whole[w], source[...], NT, preferred_element_type=F32).astype(BF16)
            local_k[s, w * Q : (w + 1) * Q, :] = tile
            if isinstance(s, int):
                recv_k[s, w * Q : (w + 1) * Q, :] = tile
                continue
            turned = tile.T

            @pl.when(w == qz)
            def _():
                recv_k[s, w * Q : (w + 1) * Q, :] = turned

            @pl.when(w != qz)
            def _():
                blocks[s, w] = turned
                block_copy(s, w).start()

    def amplitudes(s):
        for w in range(4):

            @pl.when(jnp.logical_and(s != 0, w != qz))
            def _():
                arrived(recv_k.at[s, pl.ds(w * Q, Q)], k_recv.at[s, w])

        pair_e = occ_e[orbital] + occ_e[(orbital + s) % 32]
        top = pair_e - vir_row[:, pl.ds(pl.multiple_of(qz * Q, Q), Q)]

        def one(b, _):
            rows = pl.ds(pl.multiple_of(b * Q, Q), Q)
            inverse = 1.0 / (top - vir_col[rows, :])
            k = recv_k[s, rows, :].astype(F32)
            swapped = local_k[s, rows, :].astype(F32)
            recv_k[s, rows, :] = (k * inverse).astype(BF16)
            local_k[s, rows, :] = ((2.0 * k - swapped) * inverse).astype(BF16)
            return 0

        lax.fori_loop(0, 4, one, 0)

    def product(b, s, t):
        rows = pl.ds(pl.multiple_of(b * Q, Q), Q)
        term = lax.dot_general(recv_k[s, rows, :], local_k[s], NT, preferred_element_type=F32)
        term = term + lax.dot_general(recv_k[t, rows, :], local_k[t], NT, preferred_element_type=F32)
        acc[b] = acc[b] + term.reshape(4, 4, 2, 8, NV)

    def slot_of(n):
        m = n + core
        return m + jnp.where((m == 4) | (m == 5), 2, 0) - jnp.where((m == 6) | (m == 7), 2, 0)

    integrals(0, home)
    def advance(n, _):
        slot = slot_of(n)

        @pl.when(n % 2 == 1)
        def _():
            @pl.when(n < 7)
            def _():
                l = 1 + jnp.where(n == 3, 2, 0) + jnp.where(n == 5, 1, 0)
                mine = 2 * l + core
                for ch in range(CH):
                    arrived(piece(part.at[mine], ch), p_recv.at[mine, ch])
                forward(mine, part.at[mine], l).start()

            arrived(part.at[slot], p_recv.at[slot, 0])

        integrals(slot - core, part.at[slot])
        last = jnp.where(n == 1, 0, slot_of(n - 1) - core)
        amplitudes(last)

        @pl.when(n % 2 == 0)
        def _():
            first = jnp.where(n == 2, 0, slot_of(n - 2) - core)

            def one(b, _):
                product(b, first, last)
                return 0

            lax.fori_loop(0, 4, one, 0)

        return 0

    lax.fori_loop(1, S, advance, 0)
    amplitudes(slot_of(S - 1) - core)

    def swap(g):
        rows = pl.ds(pl.multiple_of(g * 128, 128), 128)
        return remote(send0.at[rows], recv0.at[rows], c_send.at[g], c_recv.at[g], here)

    def finish(b, _):
        product(b, slot_of(S - 2) - core, slot_of(S - 1) - core)
        send0[pl.ds(pl.multiple_of(b * 128, 128), 128), :] = acc[b, :, :, other].reshape(128, NV).astype(BF16)
        swap(b).start()
        return 0

    lax.fori_loop(0, 4, finish, 0)
    started = [swap(g) for g in range(4)]

    def add_other(g, _):
        rows = pl.ds(pl.multiple_of(g * 128, 128), 128)
        swap(g).wait_recv()
        acc[g, :, :, core] = acc[g, :, :, core] + recv0[rows, :].astype(F32).reshape(4, 4, 8, NV)
        return 0

    lax.fori_loop(0, 4, add_other, 0)

    def neighbour(axis, d):
        if axis == "y":
            return device((y + d) % 4, x, z, core), (y + d) % 4
        if axis == "x":
            return device(y, (x + d) % 4, z, core), (x + d) % 4
        return device(y, x, (z + d) % 4, core), (z + d) % 4

    def first(axis, at, cols):
        if axis == "y":
            return acc[at, :, :, core, :, cols]
        if axis == "x":
            return acc[:, at, :, core, :, cols]
        return acc[:, :, at, core, :, cols]

    def exchange(stage, send, recv, take, dtype, rows, axes):
        copies = []
        for d in (1, 2, 3):
            for p, (start, width) in enumerate(PARTS):
                target, at = neighbour(axes[p], d)
                cols = pl.ds(start, width)
                send[d - 1, :, cols] = take(p, at, cols).reshape(rows, width).astype(dtype)
                sem = 9 * stage + 3 * (d - 1) + p
                copy = remote(
                    send.at[d - 1, :, cols], recv.at[d - 1, :, cols], r_send.at[sem], r_recv.at[sem], target
                )
                copy.start()
                copies.append(copy)
        started.extend(copies)
        return copies

    def total(p, take, recv, axis, cols, shape):
        _, at = neighbour(axis, 0)
        value = take(p, at, cols)
        for d in (0, 1, 2):
            value = value + recv[d, :, cols].astype(F32).reshape(shape)
        return value

    def oo_round(stage, low, targets):
        copies = []
        for n, target in enumerate(targets):
            copy = remote(
                oo_send.at[stage], oo_recv.at[low + n], g_send.at[low + n], g_recv.at[low + n], target
            )
            copy.start()
            copies.append(copy)
        started.extend(copies)
        return copies

    def sum_oo(stage, low, high):
        value = oo_send[stage]
        for index in range(low, high):
            value = value + oo_recv[index]
        return value

    axes1, axes2, axes3 = ("y", "x", "z"), ("x", "z", "y"), ("z", "y", "x")

    def take1(p, at, cols):
        return first(axes1[p], at, cols)

    def take2(p, at, cols):
        return keep1[:, at, :, cols] if p == 1 else keep1[at, :, :, cols]

    def take3(p, at, cols):
        return keep2[at, :, cols]

    round1 = exchange(0, send1, recv1, take1, BF16, 128, axes1)
    gram_acc[...] = jnp.zeros_like(gram_acc)

    def gram(g, _):
        rows = pl.ds(pl.multiple_of(g * 32, 32), 32)
        left = recv_k[:, rows, :].reshape(Q, Q)
        right = local_k[:, rows, :].reshape(Q, Q)
        gram_acc[...] += lax.dot_general(left, right, NT, preferred_element_type=F32)
        return 0

    lax.fori_loop(0, NV // 32, gram, 0)
    r = lax.broadcasted_iota(jnp.int32, (Q, Q), 0)
    c = lax.broadcasted_iota(jnp.int32, (Q, Q), 1)
    diagonal = jnp.where(r % 32 == c % 32, -gram_acc[...], 0.0)
    n = lax.broadcasted_iota(jnp.int32, (128, Q), 0)
    m = lax.broadcasted_iota(jnp.int32, (128, Q), 1)
    place = jnp.where(n == (orbital + m // 32) % 32, 1.0, 0.0).astype(F32)
    highest = lax.Precision.HIGHEST
    half = lax.dot_general(place, diagonal, (((1,), (0,)), ((), ())), precision=highest, preferred_element_type=F32)
    placed = lax.dot_general(half, place, NT, precision=highest, preferred_element_type=F32)
    oo_send[0] = placed[:32]

    for copy in round1:
        copy.wait_recv()
    for p, (start, width) in enumerate(PARTS):
        cols = pl.ds(start, width)
        keep1[:, :, :, cols] = total(p, take1, recv1, axes1[p], cols, (4, 4, 8, width))

    oo1 = oo_round(0, 0, [device((y + d) % 4, x, z, (core + e) % 2) for d in range(4) for e in range(2) if d or e])
    round2 = exchange(1, send2, recv2, take2, BF16, 32, axes2)
    for copy in round2:
        copy.wait_recv()
    for p, (start, width) in enumerate(PARTS):
        cols = pl.ds(start, width)
        keep2[:, :, cols] = total(p, take2, recv2, axes2[p], cols, (4, 8, width))

    round3 = exchange(2, send3, recv3, take3, F32, 8, axes3)
    for copy in oo1:
        copy.wait_recv()
    oo_send[1] = sum_oo(0, 0, 7)
    oo2 = oo_round(1, 7, [device(y, (x + d) % 4, (z + e) % 4, core) for d in range(4) for e in range(4) if d or e])
    for copy in round3:
        copy.wait_recv()
    for p, (start, width) in enumerate(PARTS):
        cols = pl.ds(start, width)
        vv_out[:, cols] = total(p, take3, recv3, axes3[p], cols, (8, width))
    for copy in oo2:
        copy.wait_recv()
    oo_out[...] = sum_oo(1, 7, 22)[:, :32]

    gather(1).wait_send()
    gather(3).wait_send()
    pass_on().wait_send()

    @pl.when(core != h)
    def _():
        gather(0).wait_send()
        for ch in range(CH):
            swap_home(ch).wait_send()

    for ch in range(CH):
        shift_y(ch).wait_send()
        for l in (1, 2, 3):
            along_x(l, home, ch).wait_send()
    for l in (1, 2, 3):
        forward(2 * l + core, part.at[2 * l + core], l).wait_send()
    forward(1, home, 0).wait_send()

    def drain(s, _):
        for w in range(4):

            @pl.when(w != qz)
            def _():
                block_copy(s, w).wait_send()

        return 0

    lax.fori_loop(1, S, drain, 0)
    for copy in started:
        copy.wait_send()


def on_device(factors, occupied_energy, virtual_energy):
    dma = pltpu.SemaphoreType.DMA
    vmem = pl.BlockSpec(memory_space=pltpu.VMEM)
    return pl.pallas_call(
        kernel,
        out_shape=(
            jax.ShapeDtypeStruct((8, NV), F32),
            jax.ShapeDtypeStruct((32, 32), F32),
        ),
        in_specs=[vmem, pl.BlockSpec(memory_space=pltpu.SMEM), vmem, vmem],
        out_specs=(vmem, vmem),
        scratch_shapes=[
            pltpu.VMEM((4, Q, NP), BF16),
            pltpu.VMEM((10, Q, NP), BF16),
            pltpu.VMEM((S, 4, Q, Q), BF16),
            pltpu.VMEM((S, NV, Q), BF16),
            pltpu.VMEM((S, NV, Q), BF16),
            pltpu.VMEM((4, 4, 4, 2, 8, NV), F32),
            pltpu.VMEM((Q, Q), F32),
            pltpu.VMEM((512, NV), BF16),
            pltpu.VMEM((512, NV), BF16),
            pltpu.VMEM((3, 128, NV), BF16),
            pltpu.VMEM((3, 128, NV), BF16),
            pltpu.VMEM((4, 4, 8, NV), F32),
            pltpu.VMEM((3, 32, NV), BF16),
            pltpu.VMEM((3, 32, NV), BF16),
            pltpu.VMEM((4, 8, NV), F32),
            pltpu.VMEM((3, 8, NV), F32),
            pltpu.VMEM((3, 8, NV), F32),
            pltpu.VMEM((2, 32, 128), F32),
            pltpu.VMEM((22, 32, 128), F32),
            dma((CH,)),
            dma((CH,)),
            dma((4,)),
            dma((4,)),
            dma((10, CH)),
            dma((CH,)),
            dma((4, CH)),
            dma((4,)),
            dma((S, 4)),
            dma((S, 4)),
            dma,
            dma((2,)),
            dma((4,)),
            dma((4,)),
            dma((27,)),
            dma((27,)),
            dma((22,)),
            dma((22,)),
        ],
        compiler_params=pltpu.CompilerParams(
            collective_id=0, has_side_effects=True, vmem_limit_bytes=56 * 1024 * 1024
        ),
        cost_estimate=pl.CostEstimate(
            flops=14 * 10**9, bytes_accessed=2 * 10**6, transcendentals=0
        ),
    )(factors[0], occupied_energy, virtual_energy[None, :], virtual_energy[:, None])


def solution(mesh):
    return jax.shard_map(
        on_device,
        mesh=mesh,
        in_specs=(P("occ", "vir", None), P(), P()),
        out_specs=(P(("occ", "vir"), None), P()),
        check_vma=False,
    )
```

```python
import jax
import jax.numpy as jnp
from jax import lax
from jax.experimental import pallas as pl
from jax.experimental.pallas import tpu as pltpu
from jax.sharding import PartitionSpec as P

MESH = pl.DeviceIdType.MESH
F32 = jnp.float32
BF16 = jnp.bfloat16
NT = (((1,), (1,)), ((), ()))
Q = 256
NV = 1024
NP = 2048
S = 8
CH = 4
ROWS = Q // CH
NEAR, FAR = (1, 3), (2,)
PARTS = ((0, 384), (384, 384), (768, 256))


def device(y, x, z, core):
    return ((y * 4 + x) * 2 + z // 2, (z % 2) * 2 + core)


def kernel(
    native, occ_e, vir_row, vir_col, vv_out, oo_out,
    whole, part, blocks, recv_k, local_k, acc, gram_acc,
    send0, recv0, send1, recv1, keep1, send2, recv2, keep2, send3, recv3, oo_send, oo_recv,
    h_send, h_recv, a_send, a_recv, p_recv, y_send, x_send, f_send, k_send, k_recv,
    b_send, c_send, c_recv, r_send, r_recv, g_send, g_recv,
):
    occ = lax.axis_index("occ")
    vir = lax.axis_index("vir")
    y = occ // 8
    x = (occ // 2) % 4
    h = occ % 2
    z = 2 * h + vir // 2
    core = vir % 2
    other = 1 - core
    orbital = 2 * (4 * y + x) + core

    def quarter(at):
        return 2 * (at % 2) + at // 2

    qz = quarter(z)
    here = device(y, x, z, other)

    barrier = pltpu.get_barrier_semaphore()
    peers = [here]
    for d in (1, 2, 3):
        peers.append(device((y + d) % 4, x, z, core))
        peers.append(device((y + d) % 4, x, z, other))
        peers.append(device(y, x, (z + d) % 4, core))
        peers.append(device(y, x, (z + d) % 4, other))
        for e in range(4):
            peers.append(device(y, (x + d) % 4, (z + e) % 4, core))
    for peer in peers:
        pl.semaphore_signal(barrier, inc=1, device_id=peer, device_id_type=MESH)
    pl.semaphore_wait(barrier, len(peers))

    def remote(src, dst, ssem, rsem, target):
        return pltpu.make_async_remote_copy(
            src_ref=src, dst_ref=dst, send_sem=ssem, recv_sem=rsem,
            device_id=target, device_id_type=MESH,
        )

    def arrived(ref, sem):
        pltpu.make_async_copy(ref, ref, sem).wait()

    def piece(ref, ch):
        return ref.at[pl.ds(ch * ROWS, ROWS)]

    home = whole.at[qz]
    above = part.at[8 + core]

    def swap_home(ch):
        return remote(
            piece(native, ch), piece(whole.at[vir], ch), h_send.at[ch], h_recv.at[ch],
            device(y, x, (z + 2) % 4, other),
        )

    @pl.when(core == h)
    def _():
        for ch in range(CH):
            pltpu.make_async_copy(piece(native, ch), piece(home, ch), h_recv.at[ch]).start()

    def half_of(ref, at):
        return ref.at[pl.ds(at * (Q // 2), Q // 2)]

    def gather(d, at):
        return remote(
            half_of(native, at), half_of(whole.at[vir], at), a_send.at[d, at], a_recv.at[vir, at],
            device(y, x, (z + d) % 4, h),
        )

    @pl.when(core != h)
    def _():
        for ch in range(CH):
            swap_home(ch).start()

    @pl.when(core == h)
    def _():
        gather(1, 0).start()
        gather(3, 1).start()

    place_z = (z + 4 - 2 * core) % 4
    passed = core + jnp.where(place_z % 2 == 0, 2, 0)
    distant = core + jnp.where(place_z == 3, 2, 0)
    plus = jnp.logical_and(place_z > 0, place_z < 3)
    at_passed = jnp.where(plus, 0, 1)

    def pass_on():
        ref = whole.at[passed, pl.ds(pl.multiple_of(at_passed * (Q // 2), Q // 2), Q // 2)]
        return remote(
            ref, ref, b_send, a_recv.at[passed, at_passed],
            device(y, x, jnp.where(plus, z + 1, z + 3) % 4, core),
        )

    def relay_half():
        ref = whole.at[passed, pl.ds(pl.multiple_of(at_passed * (Q // 2), Q // 2), Q // 2)]
        arrived(ref, a_recv.at[passed, at_passed])
        pass_on().start()

    def shift_y(ch):
        return remote(
            piece(home, ch), piece(above, ch), y_send.at[ch], p_recv.at[8 + core, ch],
            device((y + 3) % 4, x, z, core),
        )

    def along_x(l, src, ch):
        return remote(
            piece(src, ch), piece(part.at[2 * l + core], ch), x_send.at[l, ch], p_recv.at[2 * l + core, ch],
            device(y, (x + 4 - l) % 4, z, core),
        )

    def forward(slot, src, sem):
        return remote(src, part.at[slot], f_send.at[sem], p_recv.at[slot, 0], here)

    for ch in range(CH):
        arrived(piece(home, ch), h_recv.at[ch])
        shift_y(ch).start()
        for l in NEAR:

            @pl.when(x >= l)
            def _():
                along_x(l, home, ch).start()

    pltpu.make_async_copy(home, part.at[core], p_recv.at[core, 0]).start()

    @pl.when(core == 1)
    def _():
        forward(1, home, 0).start()

    @pl.when(core != h)
    def _():
        for at in (0, 1):
            for d in (1, 3, 0):
                gather(d, at).start()
        relay_half()

    for ch in range(CH):
        arrived(piece(above, ch), p_recv.at[8 + core, ch])
        for l in NEAR:

            @pl.when(x < l)
            def _():
                along_x(l, above, ch).start()

    @pl.when(core == h)
    def _():
        relay_half()
        gather(1, 1).start()
        gather(3, 0).start()

    @pl.when(core == 0)
    def _():
        forward(8, above, 0).start()

    def relay(l):
        mine = 2 * l + core
        for ch in range(CH):
            arrived(piece(part.at[mine], ch), p_recv.at[mine, ch])
        forward(mine, part.at[mine], l).start()

    relay(1)
    for l in FAR:

        @pl.when(x >= l)
        def _():
            for ch in range(CH):
                along_x(l, home, ch).start()

        @pl.when(x < l)
        def _():
            for ch in range(CH):
                along_x(l, above, ch).start()

    relay(3)

    rest = 1 - at_passed
    arrived(whole.at[passed, pl.ds(pl.multiple_of(rest * (Q // 2), Q // 2), Q // 2)], a_recv.at[passed, rest])
    for at in (0, 1):

        @pl.when(place_z != 2)
        def _():
            arrived(half_of(whole.at[other], at), a_recv.at[other, at])

        @pl.when(place_z != 3)
        def _():
            arrived(half_of(whole.at[2 + other], at), a_recv.at[2 + other, at])

        @pl.when(place_z >= 2)
        def _():
            arrived(half_of(whole.at[distant], at), a_recv.at[distant, at])

    def block_copy(s, w):
        return remote(
            blocks.at[s, w], recv_k.at[s, pl.ds(qz * Q, Q)], k_send.at[s, w], k_recv.at[s, qz],
            device(y, x, quarter(w), core),
        )

    def integrals(s, source):
        for w in range(4):
            tile = lax.dot_general(whole[w], source[...], NT, preferred_element_type=F32).astype(BF16)
            local_k[s, w * Q : (w + 1) * Q, :] = tile
            turned = tile.T

            @pl.when(s == 0)
            def _():
                recv_k[s, w * Q : (w + 1) * Q, :] = tile

            @pl.when(jnp.logical_and(s != 0, w == qz))
            def _():
                recv_k[s, w * Q : (w + 1) * Q, :] = turned

            @pl.when(jnp.logical_and(s != 0, w != qz))
            def _():
                blocks[s, w] = turned
                block_copy(s, w).start()

    def amplitudes(s):
        for w in range(4):

            @pl.when(jnp.logical_and(s != 0, w != qz))
            def _():
                arrived(recv_k.at[s, pl.ds(w * Q, Q)], k_recv.at[s, w])

        pair_e = occ_e[orbital] + occ_e[(orbital + s) % 32]
        top = pair_e - vir_row[:, pl.ds(pl.multiple_of(qz * Q, Q), Q)]

        def one(b, _):
            rows = pl.ds(pl.multiple_of(b * Q, Q), Q)
            inverse = 1.0 / (top - vir_col[rows, :])
            k = recv_k[s, rows, :].astype(F32)
            swapped = local_k[s, rows, :].astype(F32)
            recv_k[s, rows, :] = (k * inverse).astype(BF16)
            local_k[s, rows, :] = ((2.0 * k - swapped) * inverse).astype(BF16)
            return 0

        lax.fori_loop(0, 4, one, 0)

    def product(b, s, t):
        rows = pl.ds(pl.multiple_of(b * Q, Q), Q)
        term = lax.dot_general(recv_k[s, rows, :], local_k[s], NT, preferred_element_type=F32)
        term = term + lax.dot_general(recv_k[t, rows, :], local_k[t], NT, preferred_element_type=F32)
        acc[b] = acc[b] + term.reshape(4, 4, 2, 8, NV)

    def slot_of(n):
        near = jnp.where(n < 3, 2, 6) + (core + n + 1) % 2
        last = jnp.where(n == 5, core, 4 + (core + n) % 2)
        return jnp.where(n == 0, 1 + 7 * core, jnp.where(n < 5, near, last))

    def amplitudes_at(m):
        amplitudes(slot_of(m) - core)

    def done(n):
        return jnp.maximum(n - 1, 0) - jnp.where((n == 5) | (n == 6), 1, 0)

    def advance(n, _):
        slot = slot_of(n)

        def one(m, _):
            amplitudes_at(m)
            return 0

        lax.fori_loop(done(n - 1), done(n), one, 0)

        @pl.when((n == 3) | (n == 6) | (n == 7))
        def _():
            first, second = slot_of(done(n) - 2) - core, slot_of(done(n) - 1) - core

            def two(b, _):
                product(b, first, second)
                return 0

            lax.fori_loop(0, 4, two, 0)

        @pl.when(n == 6)
        def _():
            relay(2)

        @pl.when((n == 0) | (n == 2) | (n == 4) | (n == 5) | (n == 7))
        def _():
            arrived(part.at[slot], p_recv.at[slot, 0])

        integrals(slot - core, part.at[slot])
        return 0

    acc[...] = jnp.zeros_like(acc)
    lax.fori_loop(0, S, advance, 0)
    amplitudes_at(6)
    amplitudes_at(7)

    def swap(g):
        rows = pl.ds(pl.multiple_of(g * 128, 128), 128)
        return remote(send0.at[rows], recv0.at[rows], c_send.at[g], c_recv.at[g], here)

    def finish(b, _):
        product(b, slot_of(6) - core, slot_of(7) - core)
        send0[pl.ds(pl.multiple_of(b * 128, 128), 128), :] = acc[b, :, :, other].reshape(128, NV).astype(BF16)
        swap(b).start()
        return 0

    lax.fori_loop(0, 4, finish, 0)
    started = [swap(g) for g in range(4)]

    def add_other(g, _):
        rows = pl.ds(pl.multiple_of(g * 128, 128), 128)
        swap(g).wait_recv()
        acc[g, :, :, core] = acc[g, :, :, core] + recv0[rows, :].astype(F32).reshape(4, 4, 8, NV)
        return 0

    lax.fori_loop(0, 4, add_other, 0)

    def neighbour(axis, d):
        if axis == "y":
            return device((y + d) % 4, x, z, core), (y + d) % 4
        if axis == "x":
            return device(y, (x + d) % 4, z, core), (x + d) % 4
        return device(y, x, (z + d) % 4, core), (z + d) % 4

    def first(axis, at, cols):
        if axis == "y":
            return acc[at, :, :, core, :, cols]
        if axis == "x":
            return acc[:, at, :, core, :, cols]
        return acc[:, :, at, core, :, cols]

    def exchange(stage, send, recv, take, dtype, rows, axes):
        copies = []
        for d in (1, 2, 3):
            for p, (start, width) in enumerate(PARTS):
                target, at = neighbour(axes[p], d)
                cols = pl.ds(start, width)
                send[d - 1, :, cols] = take(p, at, cols).reshape(rows, width).astype(dtype)
                sem = 9 * stage + 3 * (d - 1) + p
                copy = remote(
                    send.at[d - 1, :, cols], recv.at[d - 1, :, cols], r_send.at[sem], r_recv.at[sem], target
                )
                copy.start()
                copies.append(copy)
        started.extend(copies)
        return copies

    def total(p, take, recv, axis, cols, shape):
        _, at = neighbour(axis, 0)
        value = take(p, at, cols)
        for d in (0, 1, 2):
            value = value + recv[d, :, cols].astype(F32).reshape(shape)
        return value

    def oo_round(stage, low, targets):
        copies = []
        for n, target in enumerate(targets):
            copy = remote(
                oo_send.at[stage], oo_recv.at[low + n], g_send.at[low + n], g_recv.at[low + n], target
            )
            copy.start()
            copies.append(copy)
        started.extend(copies)
        return copies

    def sum_oo(stage, low, high):
        value = oo_send[stage]
        for index in range(low, high):
            value = value + oo_recv[index]
        return value

    axes1, axes2, axes3 = ("y", "x", "z"), ("x", "z", "y"), ("z", "y", "x")

    def take1(p, at, cols):
        return first(axes1[p], at, cols)

    def take2(p, at, cols):
        return keep1[:, at, :, cols] if p == 1 else keep1[at, :, :, cols]

    def take3(p, at, cols):
        return keep2[at, :, cols]

    round1 = exchange(0, send1, recv1, take1, BF16, 128, axes1)
    gram_acc[...] = jnp.zeros_like(gram_acc)

    def gram(g, _):
        rows = pl.ds(pl.multiple_of(g * 32, 32), 32)
        left = recv_k[:, rows, :].reshape(Q, Q)
        right = local_k[:, rows, :].reshape(Q, Q)
        gram_acc[...] += lax.dot_general(left, right, NT, preferred_element_type=F32)
        return 0

    lax.fori_loop(0, NV // 32, gram, 0)
    r = lax.broadcasted_iota(jnp.int32, (Q, Q), 0)
    c = lax.broadcasted_iota(jnp.int32, (Q, Q), 1)
    diagonal = jnp.where(r % 32 == c % 32, -gram_acc[...], 0.0)
    n = lax.broadcasted_iota(jnp.int32, (128, Q), 0)
    m = lax.broadcasted_iota(jnp.int32, (128, Q), 1)
    place = jnp.where(n == (orbital + m // 32) % 32, 1.0, 0.0).astype(F32)
    highest = lax.Precision.HIGHEST
    half = lax.dot_general(place, diagonal, (((1,), (0,)), ((), ())), precision=highest, preferred_element_type=F32)
    placed = lax.dot_general(half, place, NT, precision=highest, preferred_element_type=F32)
    oo_send[0] = placed[:32]

    for copy in round1:
        copy.wait_recv()
    for p, (start, width) in enumerate(PARTS):
        cols = pl.ds(start, width)
        keep1[:, :, :, cols] = total(p, take1, recv1, axes1[p], cols, (4, 4, 8, width))

    oo1 = oo_round(0, 0, [device((y + d) % 4, x, z, (core + e) % 2) for d in range(4) for e in range(2) if d or e])
    round2 = exchange(1, send2, recv2, take2, BF16, 32, axes2)
    for copy in round2:
        copy.wait_recv()
    for p, (start, width) in enumerate(PARTS):
        cols = pl.ds(start, width)
        keep2[:, :, cols] = total(p, take2, recv2, axes2[p], cols, (4, 8, width))

    round3 = exchange(2, send3, recv3, take3, F32, 8, axes3)
    for copy in oo1:
        copy.wait_recv()
    oo_send[1] = sum_oo(0, 0, 7)
    oo2 = oo_round(1, 7, [device(y, (x + d) % 4, (z + e) % 4, core) for d in range(4) for e in range(4) if d or e])
    for copy in round3:
        copy.wait_recv()
    for p, (start, width) in enumerate(PARTS):
        cols = pl.ds(start, width)
        vv_out[:, cols] = total(p, take3, recv3, axes3[p], cols, (8, width))
    for copy in oo2:
        copy.wait_recv()
    oo_out[...] = sum_oo(1, 7, 22)[:, :32]

    for at in (0, 1):
        gather(1, at).wait_send()
        gather(3, at).wait_send()
    pass_on().wait_send()

    @pl.when(core != h)
    def _():
        gather(0, 0).wait_send()
        gather(0, 1).wait_send()
        for ch in range(CH):
            swap_home(ch).wait_send()

    for ch in range(CH):
        shift_y(ch).wait_send()
        for l in (1, 2, 3):
            along_x(l, home, ch).wait_send()
    for l in (1, 2, 3):
        forward(2 * l + core, part.at[2 * l + core], l).wait_send()
    forward(1, home, 0).wait_send()

    def drain(s, _):
        for w in range(4):

            @pl.when(w != qz)
            def _():
                block_copy(s, w).wait_send()

        return 0

    lax.fori_loop(1, S, drain, 0)
    for copy in started:
        copy.wait_send()


def on_device(factors, occupied_energy, virtual_energy):
    dma = pltpu.SemaphoreType.DMA
    vmem = pl.BlockSpec(memory_space=pltpu.VMEM)
    return pl.pallas_call(
        kernel,
        out_shape=(
            jax.ShapeDtypeStruct((8, NV), F32),
            jax.ShapeDtypeStruct((32, 32), F32),
        ),
        in_specs=[vmem, pl.BlockSpec(memory_space=pltpu.SMEM), vmem, vmem],
        out_specs=(vmem, vmem),
        scratch_shapes=[
            pltpu.VMEM((4, Q, NP), BF16),
            pltpu.VMEM((10, Q, NP), BF16),
            pltpu.VMEM((S, 4, Q, Q), BF16),
            pltpu.VMEM((S, NV, Q), BF16),
            pltpu.VMEM((S, NV, Q), BF16),
            pltpu.VMEM((4, 4, 4, 2, 8, NV), F32),
            pltpu.VMEM((Q, Q), F32),
            pltpu.VMEM((512, NV), BF16),
            pltpu.VMEM((512, NV), BF16),
            pltpu.VMEM((3, 128, NV), BF16),
            pltpu.VMEM((3, 128, NV), BF16),
            pltpu.VMEM((4, 4, 8, NV), F32),
            pltpu.VMEM((3, 32, NV), BF16),
            pltpu.VMEM((3, 32, NV), BF16),
            pltpu.VMEM((4, 8, NV), F32),
            pltpu.VMEM((3, 8, NV), F32),
            pltpu.VMEM((3, 8, NV), F32),
            pltpu.VMEM((2, 32, 128), F32),
            pltpu.VMEM((22, 32, 128), F32),
            dma((CH,)),
            dma((CH,)),
            dma((4, 2)),
            dma((4, 2)),
            dma((10, CH)),
            dma((CH,)),
            dma((4, CH)),
            dma((4,)),
            dma((S, 4)),
            dma((S, 4)),
            dma,
            dma((4,)),
            dma((4,)),
            dma((27,)),
            dma((27,)),
            dma((22,)),
            dma((22,)),
        ],
        compiler_params=pltpu.CompilerParams(
            collective_id=0, has_side_effects=True, vmem_limit_bytes=56 * 1024 * 1024
        ),
        cost_estimate=pl.CostEstimate(
            flops=14 * 10**9, bytes_accessed=2 * 10**6, transcendentals=0
        ),
    )(factors[0], occupied_energy, virtual_energy[None, :], virtual_energy[:, None])


def solution(mesh):
    return jax.shard_map(
        on_device,
        mesh=mesh,
        in_specs=(P("occ", "vir", None), P(), P()),
        out_specs=(P(("occ", "vir"), None), P()),
        check_vma=False,
    )
```

```python
import jax
import jax.numpy as jnp
from jax import lax
from jax.experimental import pallas as pl
from jax.experimental.pallas import tpu as pltpu
from jax.sharding import PartitionSpec as P

MESH = pl.DeviceIdType.MESH
F32 = jnp.float32
BF16 = jnp.bfloat16
NT = (((1,), (1,)), ((), ()))
Q = 256
NV = 1024
NP = 2048
S = 8
CH = 4
ROWS = Q // CH
NEAR, FAR = (1, 3), (2,)
PARTS = ((0, 384), (384, 384), (768, 256))


def device(y, x, z, core):
    return ((y * 4 + x) * 2 + z // 2, (z % 2) * 2 + core)


def kernel(
    native, occ_e, vir_row, vv_out, oo_out,
    vir_col, whole, part, blocks, recv_k, local_k, acc, gram_acc,
    send0, recv0, send1, recv1, keep1, send2, recv2, keep2, send3, recv3, oo_send, oo_recv,
    h_send, h_recv, a_send, a_recv, p_recv, y_send, x_send, f_send, k_send, k_recv,
    b_send, c_send, c_recv, r_send, r_recv, g_send, g_recv,
):
    occ = lax.axis_index("occ")
    vir = lax.axis_index("vir")
    y = occ // 8
    x = (occ // 2) % 4
    h = occ % 2
    z = 2 * h + vir // 2
    core = vir % 2
    other = 1 - core
    orbital = 2 * (4 * y + x) + core

    def quarter(at):
        return 2 * (at % 2) + at // 2

    qz = quarter(z)
    here = device(y, x, z, other)

    barrier = pltpu.get_barrier_semaphore()
    peers = [here]
    for d in (1, 2, 3):
        peers.append(device((y + d) % 4, x, z, core))
        peers.append(device((y + d) % 4, x, z, other))
        peers.append(device(y, x, (z + d) % 4, core))
        peers.append(device(y, x, (z + d) % 4, other))
        for e in range(4):
            peers.append(device(y, (x + d) % 4, (z + e) % 4, core))
    for peer in peers:
        pl.semaphore_signal(barrier, inc=1, device_id=peer, device_id_type=MESH)
    pl.semaphore_wait(barrier, len(peers))

    def remote(src, dst, ssem, rsem, target):
        return pltpu.make_async_remote_copy(
            src_ref=src, dst_ref=dst, send_sem=ssem, recv_sem=rsem,
            device_id=target, device_id_type=MESH,
        )

    def arrived(ref, sem):
        pltpu.make_async_copy(ref, ref, sem).wait()

    def piece(ref, ch):
        return ref.at[pl.ds(ch * ROWS, ROWS)]

    home = whole.at[qz]
    above = part.at[8 + core]

    def swap_home(ch):
        return remote(
            piece(native, ch), piece(whole.at[vir], ch), h_send.at[ch], h_recv.at[ch],
            device(y, x, (z + 2) % 4, other),
        )

    @pl.when(core == h)
    def _():
        for ch in range(CH):
            pltpu.make_async_copy(piece(native, ch), piece(home, ch), h_recv.at[ch]).start()

    def half_of(ref, at):
        return ref.at[pl.ds(at * (Q // 2), Q // 2)]

    def gather(d, at):
        return remote(
            half_of(native, at), half_of(whole.at[vir], at), a_send.at[d, at], a_recv.at[vir, at],
            device(y, x, (z + d) % 4, h),
        )

    @pl.when(core != h)
    def _():
        for ch in range(CH):
            swap_home(ch).start()

    @pl.when(core == h)
    def _():
        gather(1, 0).start()
        gather(3, 1).start()

    place_z = (z + 4 - 2 * core) % 4
    passed = core + jnp.where(place_z % 2 == 0, 2, 0)
    distant = core + jnp.where(place_z == 3, 2, 0)
    plus = jnp.logical_and(place_z > 0, place_z < 3)
    at_passed = jnp.where(plus, 0, 1)

    def pass_on():
        ref = whole.at[passed, pl.ds(pl.multiple_of(at_passed * (Q // 2), Q // 2), Q // 2)]
        return remote(
            ref, ref, b_send, a_recv.at[passed, at_passed],
            device(y, x, jnp.where(plus, z + 1, z + 3) % 4, core),
        )

    def relay_half():
        ref = whole.at[passed, pl.ds(pl.multiple_of(at_passed * (Q // 2), Q // 2), Q // 2)]
        arrived(ref, a_recv.at[passed, at_passed])
        pass_on().start()

    def shift_y(ch):
        return remote(
            piece(home, ch), piece(above, ch), y_send.at[ch], p_recv.at[8 + core, ch],
            device((y + 3) % 4, x, z, core),
        )

    def along_x(l, src, ch):
        return remote(
            piece(src, ch), piece(part.at[2 * l + core], ch), x_send.at[l, ch], p_recv.at[2 * l + core, ch],
            device(y, (x + 4 - l) % 4, z, core),
        )

    def forward(slot, src, sem):
        return remote(src, part.at[slot], f_send.at[sem], p_recv.at[slot, 0], here)

    for ch in range(CH):
        arrived(piece(home, ch), h_recv.at[ch])
        shift_y(ch).start()
        for l in NEAR:

            @pl.when(x >= l)
            def _():
                along_x(l, home, ch).start()

    pltpu.make_async_copy(home, part.at[core], p_recv.at[core, 0]).start()

    @pl.when(core == 1)
    def _():
        forward(1, home, 0).start()

    @pl.when(core != h)
    def _():
        for at in (0, 1):
            for d in (1, 3, 0):
                gather(d, at).start()
        relay_half()

    for ch in range(CH):
        arrived(piece(above, ch), p_recv.at[8 + core, ch])
        for l in NEAR:

            @pl.when(x < l)
            def _():
                along_x(l, above, ch).start()

    for l in FAR:

        @pl.when(x >= l)
        def _():
            for ch in range(CH):
                along_x(l, home, ch).start()

        @pl.when(x < l)
        def _():
            for ch in range(CH):
                along_x(l, above, ch).start()

    @pl.when(core == h)
    def _():
        relay_half()
        gather(1, 1).start()
        gather(3, 0).start()

    @pl.when(core == 0)
    def _():
        forward(8, above, 0).start()

    def relay(l):
        mine = 2 * l + core
        for ch in range(CH):
            arrived(piece(part.at[mine], ch), p_recv.at[mine, ch])
        forward(mine, part.at[mine], l).start()

    acc[...] = jnp.zeros_like(acc)
    vir_col[...] = jnp.broadcast_to(vir_row[...], (128, NV)).T
    rest = 1 - at_passed
    arrived(whole.at[passed, pl.ds(pl.multiple_of(rest * (Q // 2), Q // 2), Q // 2)], a_recv.at[passed, rest])
    for at in (0, 1):

        @pl.when(place_z != 2)
        def _():
            arrived(half_of(whole.at[other], at), a_recv.at[other, at])

        @pl.when(place_z != 3)
        def _():
            arrived(half_of(whole.at[2 + other], at), a_recv.at[2 + other, at])

        @pl.when(place_z >= 2)
        def _():
            arrived(half_of(whole.at[distant], at), a_recv.at[distant, at])

    def block_copy(s, w):
        return remote(
            blocks.at[s, w], recv_k.at[s, pl.ds(qz * Q, Q)], k_send.at[s, w], k_recv.at[s, qz],
            device(y, x, quarter(w), core),
        )

    def integrals(s, source):
        for w in range(4):
            tile = lax.dot_general(whole[w], source[...], NT, preferred_element_type=F32).astype(BF16)
            local_k[s, w * Q : (w + 1) * Q, :] = tile
            turned = tile.T

            @pl.when(s == 0)
            def _():
                recv_k[s, w * Q : (w + 1) * Q, :] = tile

            @pl.when(jnp.logical_and(s != 0, w == qz))
            def _():
                recv_k[s, w * Q : (w + 1) * Q, :] = turned

            @pl.when(jnp.logical_and(s != 0, w != qz))
            def _():
                blocks[s, w] = turned
                block_copy(s, w).start()

    def amplitudes(s):
        for w in range(4):

            @pl.when(jnp.logical_and(s != 0, w != qz))
            def _():
                arrived(recv_k.at[s, pl.ds(w * Q, Q)], k_recv.at[s, w])

        pair_e = occ_e[orbital] + occ_e[(orbital + s) % 32]
        top = pair_e - vir_row[:, pl.ds(pl.multiple_of(qz * Q, Q), Q)]

        def one(b, _):
            rows = pl.ds(pl.multiple_of(b * Q, Q), Q)
            column = vir_col[rows, :]
            inverse = 1.0 / (top - jnp.concatenate([column, column], axis=1))
            k = recv_k[s, rows, :].astype(F32)
            swapped = local_k[s, rows, :].astype(F32)
            recv_k[s, rows, :] = (k * inverse).astype(BF16)
            local_k[s, rows, :] = ((2.0 * k - swapped) * inverse).astype(BF16)
            return 0

        lax.fori_loop(0, 4, one, 0)

    def product(b, s, t):
        rows = pl.ds(pl.multiple_of(b * Q, Q), Q)
        term = lax.dot_general(recv_k[s, rows, :], local_k[s], NT, preferred_element_type=F32)
        term = term + lax.dot_general(recv_k[t, rows, :], local_k[t], NT, preferred_element_type=F32)
        acc[b] = acc[b] + term.reshape(4, 4, 2, 8, NV)

    def slot_of(n):
        near = jnp.where(n < 3, 2, 6) + (core + n + 1) % 2
        last = jnp.where(n == 5, core, 4 + (core + n) % 2)
        return jnp.where(n == 0, 1 + 7 * core, jnp.where(n < 5, near, last))

    def amplitudes_at(m):
        amplitudes(slot_of(m) - core)

    def done(n):
        return jnp.maximum(n - 1, 0) - jnp.where((n == 5) | (n == 6), 1, 0)

    def advance(n, _):
        slot = slot_of(n)

        def one(m, _):
            amplitudes_at(m)
            return 0

        lax.fori_loop(done(n - 1), done(n), one, 0)

        @pl.when((n == 3) | (n == 6) | (n == 7))
        def _():
            first, second = slot_of(done(n) - 2) - core, slot_of(done(n) - 1) - core

            def two(b, _):
                product(b, first, second)
                return 0

            lax.fori_loop(0, 4, two, 0)

        for step, l in ((1, 1), (3, 3), (6, 2)):

            @pl.when(n == step)
            def _():
                relay(l)

        @pl.when((n == 0) | (n == 2) | (n == 4) | (n == 5) | (n == 7))
        def _():
            arrived(part.at[slot], p_recv.at[slot, 0])

        integrals(slot - core, part.at[slot])
        return 0

    lax.fori_loop(0, S, advance, 0)
    amplitudes_at(6)
    amplitudes_at(7)

    def swap(g):
        rows = pl.ds(pl.multiple_of(g * 128, 128), 128)
        return remote(send0.at[rows], recv0.at[rows], c_send.at[g], c_recv.at[g], here)

    def finish(b, _):
        product(b, slot_of(6) - core, slot_of(7) - core)
        send0[pl.ds(pl.multiple_of(b * 128, 128), 128), :] = acc[b, :, :, other].reshape(128, NV).astype(BF16)
        swap(b).start()
        return 0

    lax.fori_loop(0, 4, finish, 0)
    started = [swap(g) for g in range(4)]

    gram_acc[...] = jnp.zeros_like(gram_acc)

    def gram(g, _):
        term = None
        for step in range(4):
            rows = pl.ds(pl.multiple_of(g * 128 + step * 32, 32), 32)
            left = recv_k[:, rows, :].reshape(Q, Q)
            right = local_k[:, rows, :].reshape(Q, Q)
            one = lax.dot_general(left, right, NT, preferred_element_type=F32)
            term = one if term is None else term + one
        gram_acc[...] += term
        return 0

    lax.fori_loop(0, NV // 128, gram, 0)

    def add_other(g, _):
        rows = pl.ds(pl.multiple_of(g * 128, 128), 128)
        swap(g).wait_recv()
        acc[g, :, :, core] = acc[g, :, :, core] + recv0[rows, :].astype(F32).reshape(4, 4, 8, NV)
        return 0

    lax.fori_loop(0, 4, add_other, 0)

    def neighbour(axis, d):
        if axis == "y":
            return device((y + d) % 4, x, z, core), (y + d) % 4
        if axis == "x":
            return device(y, (x + d) % 4, z, core), (x + d) % 4
        return device(y, x, (z + d) % 4, core), (z + d) % 4

    def first(axis, at, cols):
        if axis == "y":
            return acc[at, :, :, core, :, cols]
        if axis == "x":
            return acc[:, at, :, core, :, cols]
        return acc[:, :, at, core, :, cols]

    def exchange(stage, send, recv, take, dtype, rows, axes):
        copies = []
        for d in (1, 2, 3):
            for p, (start, width) in enumerate(PARTS):
                target, at = neighbour(axes[p], d)
                cols = pl.ds(start, width)
                send[d - 1, :, cols] = take(p, at, cols).reshape(rows, width).astype(dtype)
                sem = 9 * stage + 3 * (d - 1) + p
                copy = remote(
                    send.at[d - 1, :, cols], recv.at[d - 1, :, cols], r_send.at[sem], r_recv.at[sem], target
                )
                copy.start()
                copies.append(copy)
        started.extend(copies)
        return copies

    def total(p, take, recv, axis, cols, shape):
        _, at = neighbour(axis, 0)
        value = take(p, at, cols)
        for d in (0, 1, 2):
            value = value + recv[d, :, cols].astype(F32).reshape(shape)
        return value

    def oo_round(stage, low, targets):
        copies = []
        for n, target in enumerate(targets):
            copy = remote(
                oo_send.at[stage], oo_recv.at[low + n], g_send.at[low + n], g_recv.at[low + n], target
            )
            copy.start()
            copies.append(copy)
        started.extend(copies)
        return copies

    def sum_oo(stage, low, high):
        value = oo_send[stage]
        for index in range(low, high):
            value = value + oo_recv[index]
        return value

    axes1, axes2, axes3 = ("y", "x", "z"), ("x", "z", "y"), ("z", "y", "x")

    def take1(p, at, cols):
        return first(axes1[p], at, cols)

    def take2(p, at, cols):
        return keep1[:, at, :, cols] if p == 1 else keep1[at, :, :, cols]

    def take3(p, at, cols):
        return keep2[at, :, cols]

    round1 = exchange(0, send1, recv1, take1, BF16, 128, axes1)
    r = lax.broadcasted_iota(jnp.int32, (Q, Q), 0)
    c = lax.broadcasted_iota(jnp.int32, (Q, Q), 1)
    diagonal = jnp.where(r % 32 == c % 32, -gram_acc[...], 0.0)
    n = lax.broadcasted_iota(jnp.int32, (128, Q), 0)
    m = lax.broadcasted_iota(jnp.int32, (128, Q), 1)
    place = jnp.where(n == (orbital + m // 32) % 32, 1.0, 0.0).astype(F32)
    highest = lax.Precision.HIGHEST
    half = lax.dot_general(place, diagonal, (((1,), (0,)), ((), ())), precision=highest, preferred_element_type=F32)
    placed = lax.dot_general(half, place, NT, precision=highest, preferred_element_type=F32)
    oo_send[0] = placed[:32]

    for copy in round1:
        copy.wait_recv()
    for p, (start, width) in enumerate(PARTS):
        cols = pl.ds(start, width)
        keep1[:, :, :, cols] = total(p, take1, recv1, axes1[p], cols, (4, 4, 8, width))

    oo1 = oo_round(0, 0, [device((y + d) % 4, x, z, (core + e) % 2) for d in range(4) for e in range(2) if d or e])
    round2 = exchange(1, send2, recv2, take2, BF16, 32, axes2)
    for copy in round2:
        copy.wait_recv()
    for p, (start, width) in enumerate(PARTS):
        cols = pl.ds(start, width)
        keep2[:, :, cols] = total(p, take2, recv2, axes2[p], cols, (4, 8, width))

    round3 = exchange(2, send3, recv3, take3, F32, 8, axes3)
    for copy in oo1:
        copy.wait_recv()
    oo_send[1] = sum_oo(0, 0, 7)
    oo2 = oo_round(1, 7, [device(y, (x + d) % 4, (z + e) % 4, core) for d in range(4) for e in range(4) if d or e])
    for copy in round3:
        copy.wait_recv()
    for p, (start, width) in enumerate(PARTS):
        cols = pl.ds(start, width)
        vv_out[:, cols] = total(p, take3, recv3, axes3[p], cols, (8, width))
    for copy in oo2:
        copy.wait_recv()
    oo_out[...] = sum_oo(1, 7, 22)[:, :32]

    for at in (0, 1):
        gather(1, at).wait_send()
        gather(3, at).wait_send()
    pass_on().wait_send()

    @pl.when(core != h)
    def _():
        gather(0, 0).wait_send()
        gather(0, 1).wait_send()
        for ch in range(CH):
            swap_home(ch).wait_send()

    for ch in range(CH):
        shift_y(ch).wait_send()
        for l in (1, 2, 3):
            along_x(l, home, ch).wait_send()
    for l in (1, 2, 3):
        forward(2 * l + core, part.at[2 * l + core], l).wait_send()
    forward(1, home, 0).wait_send()

    def drain(s, _):
        for w in range(4):

            @pl.when(w != qz)
            def _():
                block_copy(s, w).wait_send()

        return 0

    lax.fori_loop(1, S, drain, 0)
    for copy in started:
        copy.wait_send()


def on_device(factors, occupied_energy, virtual_energy):
    dma = pltpu.SemaphoreType.DMA
    vmem = pl.BlockSpec(memory_space=pltpu.VMEM)
    return pl.pallas_call(
        kernel,
        out_shape=(
            jax.ShapeDtypeStruct((8, NV), F32),
            jax.ShapeDtypeStruct((32, 32), F32),
        ),
        in_specs=[pl.BlockSpec(memory_space=pl.ANY), pl.BlockSpec(memory_space=pltpu.SMEM), vmem],
        out_specs=(vmem, vmem),
        scratch_shapes=[
            pltpu.VMEM((NV, 128), F32),
            pltpu.VMEM((4, Q, NP), BF16),
            pltpu.VMEM((10, Q, NP), BF16),
            pltpu.VMEM((S, 4, Q, Q), BF16),
            pltpu.VMEM((S, NV, Q), BF16),
            pltpu.VMEM((S, NV, Q), BF16),
            pltpu.VMEM((4, 4, 4, 2, 8, NV), F32),
            pltpu.VMEM((Q, Q), F32),
            pltpu.VMEM((512, NV), BF16),
            pltpu.VMEM((512, NV), BF16),
            pltpu.VMEM((3, 128, NV), BF16),
            pltpu.VMEM((3, 128, NV), BF16),
            pltpu.VMEM((4, 4, 8, NV), F32),
            pltpu.VMEM((3, 32, NV), BF16),
            pltpu.VMEM((3, 32, NV), BF16),
            pltpu.VMEM((4, 8, NV), F32),
            pltpu.VMEM((3, 8, NV), F32),
            pltpu.VMEM((3, 8, NV), F32),
            pltpu.VMEM((2, 32, 128), F32),
            pltpu.VMEM((22, 32, 128), F32),
            dma((CH,)),
            dma((CH,)),
            dma((4, 2)),
            dma((4, 2)),
            dma((10, CH)),
            dma((CH,)),
            dma((4, CH)),
            dma((4,)),
            dma((S, 4)),
            dma((S, 4)),
            dma,
            dma((4,)),
            dma((4,)),
            dma((27,)),
            dma((27,)),
            dma((22,)),
            dma((22,)),
        ],
        compiler_params=pltpu.CompilerParams(
            collective_id=0, has_side_effects=True, vmem_limit_bytes=56 * 1024 * 1024
        ),
        cost_estimate=pl.CostEstimate(
            flops=14 * 10**9, bytes_accessed=2 * 10**6, transcendentals=0
        ),
    )(factors[0], occupied_energy, virtual_energy[None, :])


def solution(mesh):
    return jax.shard_map(
        on_device,
        mesh=mesh,
        in_specs=(P("occ", "vir", None), P(), P()),
        out_specs=(P(("occ", "vir"), None), P()),
        check_vma=False,
    )
```

```python
import jax
import jax.numpy as jnp
from jax import lax
from jax.experimental import pallas as pl
from jax.experimental.pallas import tpu as pltpu
from jax.sharding import PartitionSpec as P

MESH = pl.DeviceIdType.MESH
F32 = jnp.float32
BF16 = jnp.bfloat16
NT = (((1,), (1,)), ((), ()))
Q = 256
NV = 1024
NP = 2048
S = 8
CH = 4
ROWS = Q // CH
NEAR, FAR = (1, 3, 2), ()
PARTS = ((0, 384), (384, 384), (768, 256))


def device(y, x, z, core):
    return ((y * 4 + x) * 2 + z // 2, (z % 2) * 2 + core)


def kernel(
    native, occ_e, vir_row, vv_out, oo_out,
    vir_col, whole, part, blocks, recv_k, local_k, acc, gram_acc,
    send0, recv0, send1, recv1, keep1, send2, recv2, keep2, send3, recv3, oo_send, oo_recv,
    h_send, h_recv, a_send, a_recv, p_recv, y_send, x_send, f_send, k_send, k_recv,
    b_send, c_send, c_recv, r_send, r_recv, g_send, g_recv,
):
    occ = lax.axis_index("occ")
    vir = lax.axis_index("vir")
    y = occ // 8
    x = (occ // 2) % 4
    h = occ % 2
    z = 2 * h + vir // 2
    core = vir % 2
    other = 1 - core
    orbital = 2 * (4 * y + x) + core

    def quarter(at):
        return 2 * (at % 2) + at // 2

    qz = quarter(z)
    here = device(y, x, z, other)

    barrier = pltpu.get_barrier_semaphore()
    peers = [here]
    for d in (1, 2, 3):
        peers.append(device((y + d) % 4, x, z, core))
        peers.append(device((y + d) % 4, x, z, other))
        peers.append(device(y, x, (z + d) % 4, core))
        peers.append(device(y, x, (z + d) % 4, other))
        for e in range(4):
            peers.append(device(y, (x + d) % 4, (z + e) % 4, core))
    for peer in peers:
        pl.semaphore_signal(barrier, inc=1, device_id=peer, device_id_type=MESH)
    pl.semaphore_wait(barrier, len(peers))

    def remote(src, dst, ssem, rsem, target):
        return pltpu.make_async_remote_copy(
            src_ref=src, dst_ref=dst, send_sem=ssem, recv_sem=rsem,
            device_id=target, device_id_type=MESH,
        )

    def arrived(ref, sem):
        pltpu.make_async_copy(ref, ref, sem).wait()

    def piece(ref, ch):
        return ref.at[pl.ds(ch * ROWS, ROWS)]

    home = whole.at[qz]
    above = part.at[8 + core]

    def swap_home(ch):
        return remote(
            piece(native, ch), piece(whole.at[vir], ch), h_send.at[ch], h_recv.at[ch],
            device(y, x, (z + 2) % 4, other),
        )

    @pl.when(core == h)
    def _():
        for ch in range(CH):
            pltpu.make_async_copy(piece(native, ch), piece(home, ch), h_recv.at[ch]).start()

    def half_of(ref, at):
        return ref.at[pl.ds(at * (Q // 2), Q // 2)]

    def gather(d, at):
        return remote(
            half_of(native, at), half_of(whole.at[vir], at), a_send.at[d, at], a_recv.at[vir, at],
            device(y, x, (z + d) % 4, h),
        )

    @pl.when(core != h)
    def _():
        for ch in range(CH):
            swap_home(ch).start()

    @pl.when(core == h)
    def _():
        gather(1, 0).start()
        gather(3, 1).start()

    place_z = (z + 4 - 2 * core) % 4
    passed = core + jnp.where(place_z % 2 == 0, 2, 0)
    distant = core + jnp.where(place_z == 3, 2, 0)
    plus = jnp.logical_and(place_z > 0, place_z < 3)
    at_passed = jnp.where(plus, 0, 1)

    def pass_on():
        ref = whole.at[passed, pl.ds(pl.multiple_of(at_passed * (Q // 2), Q // 2), Q // 2)]
        return remote(
            ref, ref, b_send, a_recv.at[passed, at_passed],
            device(y, x, jnp.where(plus, z + 1, z + 3) % 4, core),
        )

    def relay_half():
        ref = whole.at[passed, pl.ds(pl.multiple_of(at_passed * (Q // 2), Q // 2), Q // 2)]
        arrived(ref, a_recv.at[passed, at_passed])
        pass_on().start()

    def shift_y(ch):
        return remote(
            piece(home, ch), piece(above, ch), y_send.at[ch], p_recv.at[8 + core, ch],
            device((y + 3) % 4, x, z, core),
        )

    def along_x(l, src, ch):
        return remote(
            piece(src, ch), piece(part.at[2 * l + core], ch), x_send.at[l, ch], p_recv.at[2 * l + core, ch],
            device(y, (x + 4 - l) % 4, z, core),
        )

    def forward(slot, src, sem):
        return remote(src, part.at[slot], f_send.at[sem], p_recv.at[slot, 0], here)

    for ch in range(CH):
        arrived(piece(home, ch), h_recv.at[ch])
        shift_y(ch).start()
        for l in NEAR:

            @pl.when(x >= l)
            def _():
                along_x(l, home, ch).start()

    pltpu.make_async_copy(home, part.at[core], p_recv.at[core, 0]).start()

    @pl.when(core == 1)
    def _():
        forward(1, home, 0).start()

    @pl.when(core != h)
    def _():
        for at in (0, 1):
            for d in (1, 3, 0):
                gather(d, at).start()
        relay_half()

    for ch in range(CH):
        arrived(piece(above, ch), p_recv.at[8 + core, ch])
        for l in NEAR:

            @pl.when(x < l)
            def _():
                along_x(l, above, ch).start()

    for l in FAR:

        @pl.when(x >= l)
        def _():
            for ch in range(CH):
                along_x(l, home, ch).start()

        @pl.when(x < l)
        def _():
            for ch in range(CH):
                along_x(l, above, ch).start()

    @pl.when(core == h)
    def _():
        relay_half()
        gather(1, 1).start()
        gather(3, 0).start()

    @pl.when(core == 0)
    def _():
        forward(8, above, 0).start()

    def relay(l):
        mine = 2 * l + core
        for ch in range(CH):
            arrived(piece(part.at[mine], ch), p_recv.at[mine, ch])
        forward(mine, part.at[mine], l).start()

    acc[...] = jnp.zeros_like(acc)
    vir_col[...] = jnp.broadcast_to(vir_row[...], (128, NV)).T
    rest = 1 - at_passed
    arrived(whole.at[passed, pl.ds(pl.multiple_of(rest * (Q // 2), Q // 2), Q // 2)], a_recv.at[passed, rest])
    for at in (0, 1):

        @pl.when(place_z != 2)
        def _():
            arrived(half_of(whole.at[other], at), a_recv.at[other, at])

        @pl.when(place_z != 3)
        def _():
            arrived(half_of(whole.at[2 + other], at), a_recv.at[2 + other, at])

        @pl.when(place_z >= 2)
        def _():
            arrived(half_of(whole.at[distant], at), a_recv.at[distant, at])

    def block_copy(s, w):
        return remote(
            blocks.at[s, w], recv_k.at[s, pl.ds(qz * Q, Q)], k_send.at[s, w], k_recv.at[s, qz],
            device(y, x, quarter(w), core),
        )

    def integrals(s, source):
        for w in range(4):
            tile = lax.dot_general(whole[w], source[...], NT, preferred_element_type=F32).astype(BF16)
            local_k[s, w * Q : (w + 1) * Q, :] = tile
            turned = tile.T

            @pl.when(s == 0)
            def _():
                recv_k[s, w * Q : (w + 1) * Q, :] = tile

            @pl.when(jnp.logical_and(s != 0, w == qz))
            def _():
                recv_k[s, w * Q : (w + 1) * Q, :] = turned

            @pl.when(jnp.logical_and(s != 0, w != qz))
            def _():
                blocks[s, w] = turned
                block_copy(s, w).start()

    def amplitudes(s):
        for w in range(4):

            @pl.when(jnp.logical_and(s != 0, w != qz))
            def _():
                arrived(recv_k.at[s, pl.ds(w * Q, Q)], k_recv.at[s, w])

        pair_e = occ_e[orbital] + occ_e[(orbital + s) % 32]
        top = pair_e - vir_row[:, pl.ds(pl.multiple_of(qz * Q, Q), Q)]

        def one(b, _):
            rows = pl.ds(pl.multiple_of(b * Q, Q), Q)
            column = vir_col[rows, :]
            inverse = 1.0 / (top - jnp.concatenate([column, column], axis=1))
            k = recv_k[s, rows, :].astype(F32)
            swapped = local_k[s, rows, :].astype(F32)
            recv_k[s, rows, :] = (k * inverse).astype(BF16)
            local_k[s, rows, :] = ((2.0 * k - swapped) * inverse).astype(BF16)
            return 0

        lax.fori_loop(0, 4, one, 0)

    def product(b, s, t):
        rows = pl.ds(pl.multiple_of(b * Q, Q), Q)
        term = lax.dot_general(recv_k[s, rows, :], local_k[s], NT, preferred_element_type=F32)
        term = term + lax.dot_general(recv_k[t, rows, :], local_k[t], NT, preferred_element_type=F32)
        acc[b] = acc[b] + term.reshape(4, 4, 2, 8, NV)

    def slot_of(n):
        near = jnp.where(n < 3, 2, 6) + (core + n + 1) % 2
        last = jnp.where(n == 5, core, 4 + (core + n) % 2)
        return jnp.where(n == 0, 1 + 7 * core, jnp.where(n < 5, near, last))

    def amplitudes_at(m):
        amplitudes(slot_of(m) - core)

    def done(n):
        return jnp.maximum(n - 1, 0) - jnp.where((n == 5) | (n == 6), 1, 0)

    def advance(n, _):
        slot = slot_of(n)

        def one(m, _):
            amplitudes_at(m)
            return 0

        lax.fori_loop(done(n - 1), done(n), one, 0)

        @pl.when((n == 3) | (n == 6) | (n == 7))
        def _():
            first, second = slot_of(done(n) - 2) - core, slot_of(done(n) - 1) - core

            def two(b, _):
                product(b, first, second)
                return 0

            lax.fori_loop(0, 4, two, 0)

        for step, l in ((1, 1), (3, 3), (6, 2)):

            @pl.when(n == step)
            def _():
                relay(l)

        @pl.when((n == 0) | (n == 2) | (n == 4) | (n == 5) | (n == 7))
        def _():
            arrived(part.at[slot], p_recv.at[slot, 0])

        integrals(slot - core, part.at[slot])
        return 0

    lax.fori_loop(0, S, advance, 0)
    def single(b, n):
        rows = pl.ds(pl.multiple_of(b * Q, Q), Q)
        s = slot_of(n) - core
        term = lax.dot_general(recv_k[s, rows, :], local_k[s], NT, preferred_element_type=F32)
        acc[b] = acc[b] + term.reshape(4, 4, 2, 8, NV)

    def sixth(b, _):
        single(b, 6)
        return 0

    amplitudes_at(6)
    lax.fori_loop(0, 4, sixth, 0)
    amplitudes_at(7)

    def swap(g):
        rows = pl.ds(pl.multiple_of(g * 128, 128), 128)
        return remote(send0.at[rows], recv0.at[rows], c_send.at[g], c_recv.at[g], here)

    def finish(b, _):
        single(b, 7)
        send0[pl.ds(pl.multiple_of(b * 128, 128), 128), :] = acc[b, :, :, other].reshape(128, NV).astype(BF16)
        swap(b).start()
        return 0

    lax.fori_loop(0, 4, finish, 0)
    started = [swap(g) for g in range(4)]

    gram_acc[...] = jnp.zeros_like(gram_acc)

    def gram(g, _):
        term = None
        for step in range(4):
            rows = pl.ds(pl.multiple_of(g * 128 + step * 32, 32), 32)
            left = recv_k[:, rows, :].reshape(Q, Q)
            right = local_k[:, rows, :].reshape(Q, Q)
            one = lax.dot_general(left, right, NT, preferred_element_type=F32)
            term = one if term is None else term + one
        gram_acc[...] += term
        return 0

    lax.fori_loop(0, NV // 128, gram, 0)

    def add_other(g, _):
        rows = pl.ds(pl.multiple_of(g * 128, 128), 128)
        swap(g).wait_recv()
        acc[g, :, :, core] = acc[g, :, :, core] + recv0[rows, :].astype(F32).reshape(4, 4, 8, NV)
        return 0

    lax.fori_loop(0, 4, add_other, 0)

    def neighbour(axis, d):
        if axis == "y":
            return device((y + d) % 4, x, z, core), (y + d) % 4
        if axis == "x":
            return device(y, (x + d) % 4, z, core), (x + d) % 4
        return device(y, x, (z + d) % 4, core), (z + d) % 4

    def first(axis, at, cols):
        if axis == "y":
            return acc[at, :, :, core, :, cols]
        if axis == "x":
            return acc[:, at, :, core, :, cols]
        return acc[:, :, at, core, :, cols]

    def exchange(stage, send, recv, take, dtype, rows, axes):
        copies = []
        for d in (1, 2, 3):
            for p, (start, width) in enumerate(PARTS):
                target, at = neighbour(axes[p], d)
                cols = pl.ds(start, width)
                send[d - 1, :, cols] = take(p, at, cols).reshape(rows, width).astype(dtype)
                sem = 9 * stage + 3 * (d - 1) + p
                copy = remote(
                    send.at[d - 1, :, cols], recv.at[d - 1, :, cols], r_send.at[sem], r_recv.at[sem], target
                )
                copy.start()
                copies.append(copy)
        started.extend(copies)
        return copies

    def total(p, take, recv, axis, cols, shape):
        _, at = neighbour(axis, 0)
        value = take(p, at, cols)
        for d in (0, 1, 2):
            value = value + recv[d, :, cols].astype(F32).reshape(shape)
        return value

    def oo_round(stage, low, targets):
        copies = []
        for n, target in enumerate(targets):
            copy = remote(
                oo_send.at[stage], oo_recv.at[low + n], g_send.at[low + n], g_recv.at[low + n], target
            )
            copy.start()
            copies.append(copy)
        started.extend(copies)
        return copies

    def sum_oo(stage, low, high):
        value = oo_send[stage]
        for index in range(low, high):
            value = value + oo_recv[index]
        return value

    axes1, axes2, axes3 = ("y", "x", "z"), ("x", "z", "y"), ("z", "y", "x")

    def take1(p, at, cols):
        return first(axes1[p], at, cols)

    def take2(p, at, cols):
        return keep1[:, at, :, cols] if p == 1 else keep1[at, :, :, cols]

    def take3(p, at, cols):
        return keep2[at, :, cols]

    round1 = exchange(0, send1, recv1, take1, BF16, 128, axes1)
    r = lax.broadcasted_iota(jnp.int32, (Q, Q), 0)
    c = lax.broadcasted_iota(jnp.int32, (Q, Q), 1)
    diagonal = jnp.where(r % 32 == c % 32, -gram_acc[...], 0.0)
    n = lax.broadcasted_iota(jnp.int32, (128, Q), 0)
    m = lax.broadcasted_iota(jnp.int32, (128, Q), 1)
    place = jnp.where(n == (orbital + m // 32) % 32, 1.0, 0.0).astype(F32)
    highest = lax.Precision.HIGHEST
    half = lax.dot_general(diagonal, place, NT, precision=highest, preferred_element_type=F32)
    half = jnp.sum(half.reshape(S, 32, 128), axis=1)
    n = lax.broadcasted_iota(jnp.int32, (32, 128), 0)
    placed = jnp.zeros((32, 128), F32)
    for s in range(S):
        placed = jnp.where(n == (orbital + s) % 32, half[s : s + 1, :], placed)
    oo_send[0] = placed

    for copy in round1:
        copy.wait_recv()
    for p, (start, width) in enumerate(PARTS):
        cols = pl.ds(start, width)
        keep1[:, :, :, cols] = total(p, take1, recv1, axes1[p], cols, (4, 4, 8, width))

    oo1 = oo_round(0, 0, [device((y + d) % 4, x, z, (core + e) % 2) for d in range(4) for e in range(2) if d or e])
    round2 = exchange(1, send2, recv2, take2, BF16, 32, axes2)
    for copy in round2:
        copy.wait_recv()
    for p, (start, width) in enumerate(PARTS):
        cols = pl.ds(start, width)
        keep2[:, :, cols] = total(p, take2, recv2, axes2[p], cols, (4, 8, width))

    round3 = exchange(2, send3, recv3, take3, F32, 8, axes3)
    for copy in oo1:
        copy.wait_recv()
    oo_send[1] = sum_oo(0, 0, 7)
    oo2 = oo_round(1, 7, [device(y, (x + d) % 4, (z + e) % 4, core) for d in range(4) for e in range(4) if d or e])
    for copy in round3:
        copy.wait_recv()
    for p, (start, width) in enumerate(PARTS):
        cols = pl.ds(start, width)
        vv_out[:, cols] = total(p, take3, recv3, axes3[p], cols, (8, width))
    for copy in oo2:
        copy.wait_recv()
    oo_out[...] = sum_oo(1, 7, 22)[:, :32]

    for at in (0, 1):
        gather(1, at).wait_send()
        gather(3, at).wait_send()
    pass_on().wait_send()

    @pl.when(core != h)
    def _():
        gather(0, 0).wait_send()
        gather(0, 1).wait_send()
        for ch in range(CH):
            swap_home(ch).wait_send()

    for ch in range(CH):
        shift_y(ch).wait_send()
        for l in (1, 2, 3):
            along_x(l, home, ch).wait_send()
    for l in (1, 2, 3):
        forward(2 * l + core, part.at[2 * l + core], l).wait_send()
    forward(1, home, 0).wait_send()

    def drain(s, _):
        for w in range(4):

            @pl.when(w != qz)
            def _():
                block_copy(s, w).wait_send()

        return 0

    lax.fori_loop(1, S, drain, 0)
    for copy in started:
        copy.wait_send()


def on_device(factors, occupied_energy, virtual_energy):
    dma = pltpu.SemaphoreType.DMA
    vmem = pl.BlockSpec(memory_space=pltpu.VMEM)
    return pl.pallas_call(
        kernel,
        out_shape=(
            jax.ShapeDtypeStruct((8, NV), F32),
            jax.ShapeDtypeStruct((32, 32), F32),
        ),
        in_specs=[pl.BlockSpec(memory_space=pl.ANY), pl.BlockSpec(memory_space=pltpu.SMEM), vmem],
        out_specs=(vmem, vmem),
        scratch_shapes=[
            pltpu.VMEM((NV, 128), F32),
            pltpu.VMEM((4, Q, NP), BF16),
            pltpu.VMEM((10, Q, NP), BF16),
            pltpu.VMEM((S, 4, Q, Q), BF16),
            pltpu.VMEM((S, NV, Q), BF16),
            pltpu.VMEM((S, NV, Q), BF16),
            pltpu.VMEM((4, 4, 4, 2, 8, NV), F32),
            pltpu.VMEM((Q, Q), F32),
            pltpu.VMEM((512, NV), BF16),
            pltpu.VMEM((512, NV), BF16),
            pltpu.VMEM((3, 128, NV), BF16),
            pltpu.VMEM((3, 128, NV), BF16),
            pltpu.VMEM((4, 4, 8, NV), F32),
            pltpu.VMEM((3, 32, NV), BF16),
            pltpu.VMEM((3, 32, NV), BF16),
            pltpu.VMEM((4, 8, NV), F32),
            pltpu.VMEM((3, 8, NV), F32),
            pltpu.VMEM((3, 8, NV), F32),
            pltpu.VMEM((2, 32, 128), F32),
            pltpu.VMEM((22, 32, 128), F32),
            dma((CH,)),
            dma((CH,)),
            dma((4, 2)),
            dma((4, 2)),
            dma((10, CH)),
            dma((CH,)),
            dma((4, CH)),
            dma((4,)),
            dma((S, 4)),
            dma((S, 4)),
            dma,
            dma((4,)),
            dma((4,)),
            dma((27,)),
            dma((27,)),
            dma((22,)),
            dma((22,)),
        ],
        compiler_params=pltpu.CompilerParams(
            collective_id=0, has_side_effects=True, vmem_limit_bytes=56 * 1024 * 1024
        ),
        cost_estimate=pl.CostEstimate(
            flops=14 * 10**9, bytes_accessed=2 * 10**6, transcendentals=0
        ),
    )(factors[0], occupied_energy, virtual_energy[None, :])


def solution(mesh):
    return jax.shard_map(
        on_device,
        mesh=mesh,
        in_specs=(P("occ", "vir", None), P(), P()),
        out_specs=(P(("occ", "vir"), None), P()),
        check_vma=False,
    )
```

```python
import jax
import jax.numpy as jnp
from jax import lax
from jax.experimental import pallas as pl
from jax.experimental.pallas import tpu as pltpu
from jax.sharding import PartitionSpec as P

MESH = pl.DeviceIdType.MESH
F32 = jnp.float32
BF16 = jnp.bfloat16
NT = (((1,), (1,)), ((), ()))
Q = 256
NV = 1024
NP = 2048
S = 8
CH = 4
ROWS = Q // CH
NEAR, FAR = (1, 3, 2), ()
PARTS = ((0, 384), (384, 384), (768, 256))


def device(y, x, z, core):
    return ((y * 4 + x) * 2 + z // 2, (z % 2) * 2 + core)


def kernel(
    native, occ_e, vir_row, vv_out, oo_out,
    vir_col, whole, part, blocks, recv_k, local_k, acc, gram_acc,
    send0, recv0, send1, recv1, keep1, send2, recv2, keep2, send3, recv3, oo_send, oo_recv,
    h_send, h_recv, a_send, a_recv, p_recv, y_send, x_send, f_send, k_send, k_recv,
    b_send, c_send, c_recv, r_send, r_recv, g_send, g_recv,
):
    occ = lax.axis_index("occ")
    vir = lax.axis_index("vir")
    y = occ // 8
    x = (occ // 2) % 4
    h = occ % 2
    z = 2 * h + vir // 2
    core = vir % 2
    other = 1 - core
    orbital = 2 * (4 * y + x) + core

    def quarter(at):
        return 2 * (at % 2) + at // 2

    qz = quarter(z)
    here = device(y, x, z, other)

    barrier = pltpu.get_barrier_semaphore()
    peers = [here]
    for d in (1, 2, 3):
        peers.append(device((y + d) % 4, x, z, core))
        peers.append(device((y + d) % 4, x, z, other))
        peers.append(device(y, x, (z + d) % 4, core))
        peers.append(device(y, x, (z + d) % 4, other))
        for e in range(4):
            peers.append(device(y, (x + d) % 4, (z + e) % 4, core))
    for peer in peers:
        pl.semaphore_signal(barrier, inc=1, device_id=peer, device_id_type=MESH)
    pl.semaphore_wait(barrier, len(peers))

    def remote(src, dst, ssem, rsem, target):
        return pltpu.make_async_remote_copy(
            src_ref=src, dst_ref=dst, send_sem=ssem, recv_sem=rsem,
            device_id=target, device_id_type=MESH,
        )

    def arrived(ref, sem):
        pltpu.make_async_copy(ref, ref, sem).wait()

    def piece(ref, ch):
        return ref.at[pl.ds(ch * ROWS, ROWS)]

    home = whole.at[qz]
    above = part.at[8 + core]

    def swap_home(ch):
        return remote(
            piece(native, ch), piece(whole.at[vir], ch), h_send.at[ch], h_recv.at[ch],
            device(y, x, (z + 2) % 4, other),
        )

    @pl.when(core == h)
    def _():
        for ch in range(CH):
            pltpu.make_async_copy(piece(native, ch), piece(home, ch), h_recv.at[ch]).start()

    def half_of(ref, at):
        return ref.at[pl.ds(at * (Q // 2), Q // 2)]

    def gather(d, at):
        return remote(
            half_of(native, at), half_of(whole.at[vir], at), a_send.at[d, at], a_recv.at[vir, at],
            device(y, x, (z + d) % 4, h),
        )

    @pl.when(core != h)
    def _():
        for ch in range(CH):
            swap_home(ch).start()

    @pl.when(core == h)
    def _():
        gather(1, 0).start()
        gather(3, 1).start()

    place_z = (z + 4 - 2 * core) % 4
    passed = core + jnp.where(place_z % 2 == 0, 2, 0)
    distant = core + jnp.where(place_z == 3, 2, 0)
    plus = jnp.logical_and(place_z > 0, place_z < 3)
    at_passed = jnp.where(plus, 0, 1)

    def pass_on():
        ref = whole.at[passed, pl.ds(pl.multiple_of(at_passed * (Q // 2), Q // 2), Q // 2)]
        return remote(
            ref, ref, b_send, a_recv.at[passed, at_passed],
            device(y, x, jnp.where(plus, z + 1, z + 3) % 4, core),
        )

    def relay_half():
        ref = whole.at[passed, pl.ds(pl.multiple_of(at_passed * (Q // 2), Q // 2), Q // 2)]
        arrived(ref, a_recv.at[passed, at_passed])
        pass_on().start()

    def shift_y(ch):
        return remote(
            piece(home, ch), piece(above, ch), y_send.at[ch], p_recv.at[8 + core, ch],
            device((y + 3) % 4, x, z, core),
        )

    def along_x(l, src, ch):
        return remote(
            piece(src, ch), piece(part.at[2 * l + core], ch), x_send.at[l, ch], p_recv.at[2 * l + core, ch],
            device(y, (x + 4 - l) % 4, z, core),
        )

    def forward(slot, src, sem):
        return remote(src, part.at[slot], f_send.at[sem], p_recv.at[slot, 0], here)

    for ch in range(CH):
        arrived(piece(home, ch), h_recv.at[ch])
        shift_y(ch).start()
        for l in NEAR:

            @pl.when(x >= l)
            def _():
                along_x(l, home, ch).start()

    pltpu.make_async_copy(home, part.at[core], p_recv.at[core, 0]).start()

    @pl.when(core == 1)
    def _():
        forward(1, home, 0).start()

    @pl.when(core != h)
    def _():
        for at in (0, 1):
            for d in (1, 3, 0):
                gather(d, at).start()
        relay_half()

    for ch in range(CH):
        arrived(piece(above, ch), p_recv.at[8 + core, ch])
        for l in NEAR:

            @pl.when(x < l)
            def _():
                along_x(l, above, ch).start()

    for l in FAR:

        @pl.when(x >= l)
        def _():
            for ch in range(CH):
                along_x(l, home, ch).start()

        @pl.when(x < l)
        def _():
            for ch in range(CH):
                along_x(l, above, ch).start()

    @pl.when(core == h)
    def _():
        relay_half()
        gather(1, 1).start()
        gather(3, 0).start()

    @pl.when(core == 0)
    def _():
        forward(8, above, 0).start()

    def relay(l):
        mine = 2 * l + core
        for ch in range(CH):
            arrived(piece(part.at[mine], ch), p_recv.at[mine, ch])
        forward(mine, part.at[mine], l).start()

    acc[...] = jnp.zeros_like(acc)
    vir_col[...] = jnp.broadcast_to(vir_row[...], (128, NV)).T
    rest = 1 - at_passed
    arrived(whole.at[passed, pl.ds(pl.multiple_of(rest * (Q // 2), Q // 2), Q // 2)], a_recv.at[passed, rest])
    for at in (0, 1):

        @pl.when(place_z != 2)
        def _():
            arrived(half_of(whole.at[other], at), a_recv.at[other, at])

        @pl.when(place_z != 3)
        def _():
            arrived(half_of(whole.at[2 + other], at), a_recv.at[2 + other, at])

        @pl.when(place_z >= 2)
        def _():
            arrived(half_of(whole.at[distant], at), a_recv.at[distant, at])

    def block_copy(s, w):
        return remote(
            blocks.at[s, w], recv_k.at[s, pl.ds(qz * Q, Q)], k_send.at[s, w], k_recv.at[s, qz],
            device(y, x, quarter(w), core),
        )

    def integrals(s, source):
        for w in range(4):
            tile = lax.dot_general(whole[w], source[...], NT, preferred_element_type=F32).astype(BF16)
            local_k[s, w * Q : (w + 1) * Q, :] = tile
            turned = tile.T

            @pl.when(s == 0)
            def _():
                recv_k[s, w * Q : (w + 1) * Q, :] = tile

            @pl.when(jnp.logical_and(s != 0, w == qz))
            def _():
                recv_k[s, w * Q : (w + 1) * Q, :] = turned

            @pl.when(jnp.logical_and(s != 0, w != qz))
            def _():
                blocks[s, w] = turned
                block_copy(s, w).start()

    def amplitudes(s):
        for w in range(4):

            @pl.when(jnp.logical_and(s != 0, w != qz))
            def _():
                arrived(recv_k.at[s, pl.ds(w * Q, Q)], k_recv.at[s, w])

        pair_e = occ_e[orbital] + occ_e[(orbital + s) % 32]
        top = pair_e - vir_row[:, pl.ds(pl.multiple_of(qz * Q, Q), Q)]

        def one(b, _):
            rows = pl.ds(pl.multiple_of(b * Q, Q), Q)
            column = vir_col[rows, :]
            inverse = 1.0 / (top - jnp.concatenate([column, column], axis=1))
            k = recv_k[s, rows, :].astype(F32)
            swapped = local_k[s, rows, :].astype(F32)
            recv_k[s, rows, :] = (k * inverse).astype(BF16)
            local_k[s, rows, :] = ((2.0 * k - swapped) * inverse).astype(BF16)
            return 0

        lax.fori_loop(0, 4, one, 0)

    def product(b, s, t):
        rows = pl.ds(pl.multiple_of(b * Q, Q), Q)
        term = lax.dot_general(recv_k[s, rows, :], local_k[s], NT, preferred_element_type=F32)
        term = term + lax.dot_general(recv_k[t, rows, :], local_k[t], NT, preferred_element_type=F32)
        acc[b] = acc[b] + term.reshape(4, 4, 2, 8, NV)

    def slot_of(n):
        near = jnp.where(n < 3, 2, 6) + (core + n + 1) % 2
        last = jnp.where(n == 5, core, 4 + (core + n) % 2)
        return jnp.where(n == 0, 1 + 7 * core, jnp.where(n < 5, near, last))

    def amplitudes_at(m):
        amplitudes(slot_of(m) - core)

    def done(n):
        return jnp.maximum(n - 1, 0) - jnp.where((n == 5) | (n == 6), 1, 0)

    def advance(n, _):
        slot = slot_of(n)

        def one(m, _):
            amplitudes_at(m)
            return 0

        lax.fori_loop(done(n - 1), done(n), one, 0)

        @pl.when((n == 3) | (n == 6) | (n == 7))
        def _():
            first, second = slot_of(done(n) - 2) - core, slot_of(done(n) - 1) - core

            def two(b, _):
                product(b, first, second)
                return 0

            lax.fori_loop(0, 4, two, 0)

        for step, l in ((1, 1), (3, 3), (6, 2)):

            @pl.when(n == step)
            def _():
                relay(l)

        @pl.when((n == 0) | (n == 2) | (n == 4) | (n == 5) | (n == 7))
        def _():
            arrived(part.at[slot], p_recv.at[slot, 0])

        integrals(slot - core, part.at[slot])
        return 0

    lax.fori_loop(0, S, advance, 0)
    def single(b, n):
        rows = pl.ds(pl.multiple_of(b * Q, Q), Q)
        s = slot_of(n) - core
        term = lax.dot_general(recv_k[s, rows, :], local_k[s], NT, preferred_element_type=F32)
        acc[b] = acc[b] + term.reshape(4, 4, 2, 8, NV)

    def sixth(b, _):
        single(b, 6)
        return 0

    amplitudes_at(6)
    lax.fori_loop(0, 4, sixth, 0)
    amplitudes_at(7)

    def swap(g):
        rows = pl.ds(pl.multiple_of(g * 128, 128), 128)
        return remote(send0.at[rows], recv0.at[rows], c_send.at[g], c_recv.at[g], here)

    def finish(b, _):
        single(b, 7)
        send0[pl.ds(pl.multiple_of(b * 128, 128), 128), :] = acc[b, :, :, other].reshape(128, NV).astype(BF16)
        swap(b).start()
        return 0

    lax.fori_loop(0, 4, finish, 0)
    started = [swap(g) for g in range(4)]

    gram_acc[...] = jnp.zeros_like(gram_acc)

    def gram(g, _):
        term = None
        for step in range(4):
            rows = pl.ds(pl.multiple_of(g * 128 + step * 32, 32), 32)
            left = recv_k[:, rows, :].reshape(Q, Q)
            right = local_k[:, rows, :].reshape(Q, Q)
            one = lax.dot_general(left, right, NT, preferred_element_type=F32)
            term = one if term is None else term + one
        gram_acc[...] += term
        return 0

    def add_other(g, _):
        rows = pl.ds(pl.multiple_of(g * 128, 128), 128)
        swap(g).wait_recv()
        acc[g, :, :, core] = acc[g, :, :, core] + recv0[rows, :].astype(F32).reshape(4, 4, 8, NV)
        return 0

    lax.fori_loop(0, 4, add_other, 0)

    def neighbour(axis, d):
        if axis == "y":
            return device((y + d) % 4, x, z, core), (y + d) % 4
        if axis == "x":
            return device(y, (x + d) % 4, z, core), (x + d) % 4
        return device(y, x, (z + d) % 4, core), (z + d) % 4

    def first(axis, at, cols):
        if axis == "y":
            return acc[at, :, :, core, :, cols]
        if axis == "x":
            return acc[:, at, :, core, :, cols]
        return acc[:, :, at, core, :, cols]

    def exchange(stage, send, recv, take, dtype, rows, axes):
        copies = []
        for d in (1, 2, 3):
            for p, (start, width) in enumerate(PARTS):
                target, at = neighbour(axes[p], d)
                cols = pl.ds(start, width)
                send[d - 1, :, cols] = take(p, at, cols).reshape(rows, width).astype(dtype)
                sem = 9 * stage + 3 * (d - 1) + p
                copy = remote(
                    send.at[d - 1, :, cols], recv.at[d - 1, :, cols], r_send.at[sem], r_recv.at[sem], target
                )
                copy.start()
                copies.append(copy)
        started.extend(copies)
        return copies

    def total(p, take, recv, axis, cols, shape):
        _, at = neighbour(axis, 0)
        value = take(p, at, cols)
        for d in (0, 1, 2):
            value = value + recv[d, :, cols].astype(F32).reshape(shape)
        return value

    def oo_round(stage, low, targets):
        copies = []
        for n, target in enumerate(targets):
            copy = remote(
                oo_send.at[stage], oo_recv.at[low + n], g_send.at[low + n], g_recv.at[low + n], target
            )
            copy.start()
            copies.append(copy)
        started.extend(copies)
        return copies

    def sum_oo(stage, low, high):
        value = oo_send[stage]
        for index in range(low, high):
            value = value + oo_recv[index]
        return value

    axes1, axes2, axes3 = ("y", "x", "z"), ("x", "z", "y"), ("z", "y", "x")

    def take1(p, at, cols):
        return first(axes1[p], at, cols)

    def take2(p, at, cols):
        return keep1[:, at, :, cols] if p == 1 else keep1[at, :, :, cols]

    def take3(p, at, cols):
        return keep2[at, :, cols]

    round1 = exchange(0, send1, recv1, take1, BF16, 128, axes1)
    lax.fori_loop(0, NV // 128, gram, 0)
    r = lax.broadcasted_iota(jnp.int32, (Q, Q), 0)
    c = lax.broadcasted_iota(jnp.int32, (Q, Q), 1)
    diagonal = jnp.where(r % 32 == c % 32, -gram_acc[...], 0.0)
    n = lax.broadcasted_iota(jnp.int32, (128, Q), 0)
    m = lax.broadcasted_iota(jnp.int32, (128, Q), 1)
    place = jnp.where(n == (orbital + m // 32) % 32, 1.0, 0.0).astype(F32)
    highest = lax.Precision.HIGHEST
    half = lax.dot_general(diagonal, place, NT, precision=highest, preferred_element_type=F32)
    half = jnp.sum(half.reshape(S, 32, 128), axis=1)
    n = lax.broadcasted_iota(jnp.int32, (32, 128), 0)
    placed = jnp.zeros((32, 128), F32)
    for s in range(S):
        placed = jnp.where(n == (orbital + s) % 32, half[s : s + 1, :], placed)
    oo_send[0] = placed

    for copy in round1:
        copy.wait_recv()
    for p, (start, width) in enumerate(PARTS):
        cols = pl.ds(start, width)
        keep1[:, :, :, cols] = total(p, take1, recv1, axes1[p], cols, (4, 4, 8, width))

    oo1 = oo_round(0, 0, [device((y + d) % 4, x, z, (core + e) % 2) for d in range(4) for e in range(2) if d or e])
    round2 = exchange(1, send2, recv2, take2, BF16, 32, axes2)
    for copy in round2:
        copy.wait_recv()
    for p, (start, width) in enumerate(PARTS):
        cols = pl.ds(start, width)
        keep2[:, :, cols] = total(p, take2, recv2, axes2[p], cols, (4, 8, width))

    round3 = exchange(2, send3, recv3, take3, F32, 8, axes3)
    for copy in oo1:
        copy.wait_recv()
    oo_send[1] = sum_oo(0, 0, 7)
    oo2 = oo_round(1, 7, [device(y, (x + d) % 4, (z + e) % 4, core) for d in range(4) for e in range(4) if d or e])
    for copy in round3:
        copy.wait_recv()
    for p, (start, width) in enumerate(PARTS):
        cols = pl.ds(start, width)
        vv_out[:, cols] = total(p, take3, recv3, axes3[p], cols, (8, width))
    for copy in oo2:
        copy.wait_recv()
    oo_out[...] = sum_oo(1, 7, 22)[:, :32]

    for at in (0, 1):
        gather(1, at).wait_send()
        gather(3, at).wait_send()
    pass_on().wait_send()

    @pl.when(core != h)
    def _():
        gather(0, 0).wait_send()
        gather(0, 1).wait_send()
        for ch in range(CH):
            swap_home(ch).wait_send()

    for ch in range(CH):
        shift_y(ch).wait_send()
        for l in (1, 2, 3):
            along_x(l, home, ch).wait_send()
    for l in (1, 2, 3):
        forward(2 * l + core, part.at[2 * l + core], l).wait_send()
    forward(1, home, 0).wait_send()

    def drain(s, _):
        for w in range(4):

            @pl.when(w != qz)
            def _():
                block_copy(s, w).wait_send()

        return 0

    lax.fori_loop(1, S, drain, 0)
    for copy in started:
        copy.wait_send()


def on_device(factors, occupied_energy, virtual_energy):
    dma = pltpu.SemaphoreType.DMA
    vmem = pl.BlockSpec(memory_space=pltpu.VMEM)
    return pl.pallas_call(
        kernel,
        out_shape=(
            jax.ShapeDtypeStruct((8, NV), F32),
            jax.ShapeDtypeStruct((32, 32), F32),
        ),
        in_specs=[pl.BlockSpec(memory_space=pl.ANY), pl.BlockSpec(memory_space=pltpu.SMEM), vmem],
        out_specs=(vmem, vmem),
        scratch_shapes=[
            pltpu.VMEM((NV, 128), F32),
            pltpu.VMEM((4, Q, NP), BF16),
            pltpu.VMEM((10, Q, NP), BF16),
            pltpu.VMEM((S, 4, Q, Q), BF16),
            pltpu.VMEM((S, NV, Q), BF16),
            pltpu.VMEM((S, NV, Q), BF16),
            pltpu.VMEM((4, 4, 4, 2, 8, NV), F32),
            pltpu.VMEM((Q, Q), F32),
            pltpu.VMEM((512, NV), BF16),
            pltpu.VMEM((512, NV), BF16),
            pltpu.VMEM((3, 128, NV), BF16),
            pltpu.VMEM((3, 128, NV), BF16),
            pltpu.VMEM((4, 4, 8, NV), F32),
            pltpu.VMEM((3, 32, NV), BF16),
            pltpu.VMEM((3, 32, NV), BF16),
            pltpu.VMEM((4, 8, NV), F32),
            pltpu.VMEM((3, 8, NV), F32),
            pltpu.VMEM((3, 8, NV), F32),
            pltpu.VMEM((2, 32, 128), F32),
            pltpu.VMEM((22, 32, 128), F32),
            dma((CH,)),
            dma((CH,)),
            dma((4, 2)),
            dma((4, 2)),
            dma((10, CH)),
            dma((CH,)),
            dma((4, CH)),
            dma((4,)),
            dma((S, 4)),
            dma((S, 4)),
            dma,
            dma((4,)),
            dma((4,)),
            dma((27,)),
            dma((27,)),
            dma((22,)),
            dma((22,)),
        ],
        compiler_params=pltpu.CompilerParams(
            collective_id=0, has_side_effects=True, vmem_limit_bytes=56 * 1024 * 1024
        ),
        cost_estimate=pl.CostEstimate(
            flops=14 * 10**9, bytes_accessed=2 * 10**6, transcendentals=0
        ),
    )(factors[0], occupied_energy, virtual_energy[None, :])


def solution(mesh):
    return jax.shard_map(
        on_device,
        mesh=mesh,
        in_specs=(P("occ", "vir", None), P(), P()),
        out_specs=(P(("occ", "vir"), None), P()),
        check_vma=False,
    )
```

```python
import jax
import jax.numpy as jnp
from jax import lax
from jax.experimental import pallas as pl
from jax.experimental.pallas import tpu as pltpu
from jax.sharding import PartitionSpec as P

MESH = pl.DeviceIdType.MESH
F32 = jnp.float32
BF16 = jnp.bfloat16
NT = (((1,), (1,)), ((), ()))
Q = 256
NV = 1024
NP = 2048
S = 8
CH = 4
ROWS = Q // CH
NEAR, FAR = (1, 3, 2), ()
PARTS = ((0, 384), (384, 384), (768, 256))


def device(y, x, z, core):
    return ((y * 4 + x) * 2 + z // 2, (z % 2) * 2 + core)


def kernel(
    native, occ_e, vir_row, vv_out, oo_out,
    vir_col, whole, part, blocks, recv_k, local_k, acc, gram_acc,
    send0, recv0, send1, recv1, keep1, send2, recv2, keep2, send3, recv3, oo_send, oo_recv,
    h_send, h_recv, a_send, a_recv, p_recv, y_send, x_send, f_send, k_send, k_recv,
    b_send, c_send, c_recv, r_send, r_recv, g_send, g_recv,
):
    occ = lax.axis_index("occ")
    vir = lax.axis_index("vir")
    y = occ // 8
    x = (occ // 2) % 4
    h = occ % 2
    z = 2 * h + vir // 2
    core = vir % 2
    other = 1 - core
    orbital = 2 * (4 * y + x) + core

    def quarter(at):
        return 2 * (at % 2) + at // 2

    qz = quarter(z)
    here = device(y, x, z, other)

    barrier = pltpu.get_barrier_semaphore()
    peers = [here]
    for d in (1, 2, 3):
        peers.append(device((y + d) % 4, x, z, core))
        peers.append(device((y + d) % 4, x, z, other))
        peers.append(device(y, x, (z + d) % 4, core))
        peers.append(device(y, x, (z + d) % 4, other))
        for e in range(4):
            peers.append(device(y, (x + d) % 4, (z + e) % 4, core))
    for peer in peers:
        pl.semaphore_signal(barrier, inc=1, device_id=peer, device_id_type=MESH)
    pl.semaphore_wait(barrier, len(peers))

    def remote(src, dst, ssem, rsem, target):
        return pltpu.make_async_remote_copy(
            src_ref=src, dst_ref=dst, send_sem=ssem, recv_sem=rsem,
            device_id=target, device_id_type=MESH,
        )

    def arrived(ref, sem):
        pltpu.make_async_copy(ref, ref, sem).wait()

    def piece(ref, ch):
        return ref.at[pl.ds(ch * ROWS, ROWS)]

    home = whole.at[qz]
    above = part.at[8 + core]

    def swap_home(ch):
        return remote(
            piece(native, ch), piece(whole.at[vir], ch), h_send.at[ch], h_recv.at[ch],
            device(y, x, (z + 2) % 4, other),
        )

    @pl.when(core == h)
    def _():
        for ch in range(CH):
            pltpu.make_async_copy(piece(native, ch), piece(home, ch), h_recv.at[ch]).start()

    def half_of(ref, at):
        return ref.at[pl.ds(at * (Q // 2), Q // 2)]

    def gather(d, at):
        return remote(
            half_of(native, at), half_of(whole.at[vir], at), a_send.at[d, at], a_recv.at[vir, at],
            device(y, x, (z + d) % 4, h),
        )

    @pl.when(core != h)
    def _():
        for ch in range(CH):
            swap_home(ch).start()

    @pl.when(core == h)
    def _():
        gather(1, 0).start()
        gather(3, 1).start()

    place_z = (z + 4 - 2 * core) % 4
    passed = core + jnp.where(place_z % 2 == 0, 2, 0)
    distant = core + jnp.where(place_z == 3, 2, 0)
    plus = jnp.logical_and(place_z > 0, place_z < 3)
    at_passed = jnp.where(plus, 0, 1)

    def pass_on():
        ref = whole.at[passed, pl.ds(pl.multiple_of(at_passed * (Q // 2), Q // 2), Q // 2)]
        return remote(
            ref, ref, b_send, a_recv.at[passed, at_passed],
            device(y, x, jnp.where(plus, z + 1, z + 3) % 4, core),
        )

    def relay_half():
        ref = whole.at[passed, pl.ds(pl.multiple_of(at_passed * (Q // 2), Q // 2), Q // 2)]
        arrived(ref, a_recv.at[passed, at_passed])
        pass_on().start()

    def shift_y(ch):
        return remote(
            piece(home, ch), piece(above, ch), y_send.at[ch], p_recv.at[8 + core, ch],
            device((y + 3) % 4, x, z, core),
        )

    def along_x(l, src, ch):
        return remote(
            piece(src, ch), piece(part.at[2 * l + core], ch), x_send.at[l, ch], p_recv.at[2 * l + core, ch],
            device(y, (x + 4 - l) % 4, z, core),
        )

    def forward(slot, src, sem):
        return remote(src, part.at[slot], f_send.at[sem], p_recv.at[slot, 0], here)

    for ch in range(CH):
        arrived(piece(home, ch), h_recv.at[ch])
        shift_y(ch).start()
        for l in NEAR:

            @pl.when(x >= l)
            def _():
                along_x(l, home, ch).start()

    pltpu.make_async_copy(home, part.at[core], p_recv.at[core, 0]).start()

    @pl.when(core == 1)
    def _():
        forward(1, home, 0).start()

    @pl.when(core != h)
    def _():
        for at in (0, 1):
            for d in (1, 3, 0):
                gather(d, at).start()
        relay_half()

    for ch in range(CH):
        arrived(piece(above, ch), p_recv.at[8 + core, ch])
        for l in NEAR:

            @pl.when(x < l)
            def _():
                along_x(l, above, ch).start()

    for l in FAR:

        @pl.when(x >= l)
        def _():
            for ch in range(CH):
                along_x(l, home, ch).start()

        @pl.when(x < l)
        def _():
            for ch in range(CH):
                along_x(l, above, ch).start()

    @pl.when(core == h)
    def _():
        relay_half()
        gather(1, 1).start()
        gather(3, 0).start()

    @pl.when(core == 0)
    def _():
        forward(8, above, 0).start()

    def relay(l):
        mine = 2 * l + core
        for ch in range(CH):
            arrived(piece(part.at[mine], ch), p_recv.at[mine, ch])
        forward(mine, part.at[mine], l).start()

    acc[...] = jnp.zeros_like(acc)
    vir_col[...] = jnp.broadcast_to(vir_row[...], (128, NV)).T
    rest = 1 - at_passed
    arrived(whole.at[passed, pl.ds(pl.multiple_of(rest * (Q // 2), Q // 2), Q // 2)], a_recv.at[passed, rest])
    for at in (0, 1):

        @pl.when(place_z != 2)
        def _():
            arrived(half_of(whole.at[other], at), a_recv.at[other, at])

        @pl.when(place_z != 3)
        def _():
            arrived(half_of(whole.at[2 + other], at), a_recv.at[2 + other, at])

        @pl.when(place_z >= 2)
        def _():
            arrived(half_of(whole.at[distant], at), a_recv.at[distant, at])

    def block_copy(s, w):
        return remote(
            blocks.at[s, w], recv_k.at[s, pl.ds(qz * Q, Q)], k_send.at[s, w], k_recv.at[s, qz],
            device(y, x, quarter(w), core),
        )

    def integrals(s, source):
        for w in range(4):
            tile = lax.dot_general(whole[w], source[...], NT, preferred_element_type=F32).astype(BF16)
            local_k[s, w * Q : (w + 1) * Q, :] = tile
            turned = tile.T

            @pl.when(s == 0)
            def _():
                recv_k[s, w * Q : (w + 1) * Q, :] = tile

            @pl.when(jnp.logical_and(s != 0, w == qz))
            def _():
                recv_k[s, w * Q : (w + 1) * Q, :] = turned

            @pl.when(jnp.logical_and(s != 0, w != qz))
            def _():
                blocks[s, w] = turned
                block_copy(s, w).start()

    def amplitudes(s):
        for w in range(4):

            @pl.when(jnp.logical_and(s != 0, w != qz))
            def _():
                arrived(recv_k.at[s, pl.ds(w * Q, Q)], k_recv.at[s, w])

        pair_e = occ_e[orbital] + occ_e[(orbital + s) % 32]
        top = pair_e - vir_row[:, pl.ds(pl.multiple_of(qz * Q, Q), Q)]

        def one(b, _):
            rows = pl.ds(pl.multiple_of(b * Q, Q), Q)
            column = vir_col[rows, :]
            inverse = 1.0 / (top - jnp.concatenate([column, column], axis=1))
            k = recv_k[s, rows, :].astype(F32)
            swapped = local_k[s, rows, :].astype(F32)
            recv_k[s, rows, :] = (k * inverse).astype(BF16)
            local_k[s, rows, :] = ((2.0 * k - swapped) * inverse).astype(BF16)
            return 0

        lax.fori_loop(0, 4, one, 0)

    def product(b, s, t):
        rows = pl.ds(pl.multiple_of(b * Q, Q), Q)
        term = lax.dot_general(recv_k[s, rows, :], local_k[s], NT, preferred_element_type=F32)
        term = term + lax.dot_general(recv_k[t, rows, :], local_k[t], NT, preferred_element_type=F32)
        acc[b] = acc[b] + term.reshape(4, 4, 2, 8, NV)

    def slot_of(n):
        near = jnp.where(n < 3, 2, 6) + (core + n + 1) % 2
        last = jnp.where(n == 5, core, 4 + (core + n) % 2)
        return jnp.where(n == 0, 1 + 7 * core, jnp.where(n < 5, near, last))

    def amplitudes_at(m):
        amplitudes(slot_of(m) - core)

    def done(n):
        return jnp.maximum(n - 1, 0) - jnp.where((n == 5) | (n == 6), 1, 0)

    def advance(n, _):
        slot = slot_of(n)

        def one(m, _):
            amplitudes_at(m)
            return 0

        lax.fori_loop(done(n - 1), done(n), one, 0)

        @pl.when((n == 3) | (n == 6) | (n == 7))
        def _():
            first, second = slot_of(done(n) - 2) - core, slot_of(done(n) - 1) - core

            def two(b, _):
                product(b, first, second)
                return 0

            lax.fori_loop(0, 4, two, 0)

        for step, l in ((1, 1), (3, 3), (6, 2)):

            @pl.when(n == step)
            def _():
                relay(l)

        @pl.when((n == 0) | (n == 2) | (n == 4) | (n == 5) | (n == 7))
        def _():
            arrived(part.at[slot], p_recv.at[slot, 0])

        integrals(slot - core, part.at[slot])
        return 0

    lax.fori_loop(0, S, advance, 0)
    def single(b, n):
        rows = pl.ds(pl.multiple_of(b * Q, Q), Q)
        s = slot_of(n) - core
        term = lax.dot_general(recv_k[s, rows, :], local_k[s], NT, preferred_element_type=F32)
        acc[b] = acc[b] + term.reshape(4, 4, 2, 8, NV)

    def sixth(b, _):
        single(b, 6)
        return 0

    amplitudes_at(6)
    lax.fori_loop(0, 4, sixth, 0)
    amplitudes_at(7)

    def swap(g):
        rows = pl.ds(pl.multiple_of(g * 128, 128), 128)
        return remote(send0.at[rows], recv0.at[rows], c_send.at[g], c_recv.at[g], here)

    def finish(step, _):
        b = (y + 1 + step) % 4
        single(b, 7)
        send0[pl.ds(pl.multiple_of(b * 128, 128), 128), :] = acc[b, :, :, other].reshape(128, NV).astype(BF16)
        swap(b).start()
        return 0

    lax.fori_loop(0, 4, finish, 0)
    started = [swap(g) for g in range(4)]

    gram_acc[...] = jnp.zeros_like(gram_acc)

    def gram(g, _):
        term = None
        for step in range(4):
            rows = pl.ds(pl.multiple_of(g * 128 + step * 32, 32), 32)
            left = recv_k[:, rows, :].reshape(Q, Q)
            right = local_k[:, rows, :].reshape(Q, Q)
            one = lax.dot_general(left, right, NT, preferred_element_type=F32)
            term = one if term is None else term + one
        gram_acc[...] += term
        return 0

    def neighbour(axis, d):
        if axis == "y":
            return device((y + d) % 4, x, z, core), (y + d) % 4
        if axis == "x":
            return device(y, (x + d) % 4, z, core), (x + d) % 4
        return device(y, x, (z + d) % 4, core), (z + d) % 4

    def first(axis, at, cols):
        if axis == "y":
            return acc[at, :, :, core, :, cols]
        if axis == "x":
            return acc[:, at, :, core, :, cols]
        return acc[:, :, at, core, :, cols]

    def exchange(stage, send, recv, take, dtype, rows, axes, parts=(0, 1, 2)):
        copies = []
        for d in (1, 2, 3):
            for p in parts:
                copies.append(deliver(stage, send, recv, take, dtype, rows, axes, d, p))
        return copies

    def deliver(stage, send, recv, take, dtype, rows, axes, d, p):
        start, width = PARTS[p]
        target, at = neighbour(axes[p], d)
        cols = pl.ds(start, width)
        send[d - 1, :, cols] = take(p, at, cols).reshape(rows, width).astype(dtype)
        sem = 9 * stage + 3 * (d - 1) + p
        copy = remote(send.at[d - 1, :, cols], recv.at[d - 1, :, cols], r_send.at[sem], r_recv.at[sem], target)
        copy.start()
        started.append(copy)
        return copy

    def total(p, take, recv, axis, cols, shape):
        _, at = neighbour(axis, 0)
        value = take(p, at, cols)
        for d in (0, 1, 2):
            value = value + recv[d, :, cols].astype(F32).reshape(shape)
        return value

    def oo_round(stage, low, targets):
        copies = []
        for n, target in enumerate(targets):
            copy = remote(
                oo_send.at[stage], oo_recv.at[low + n], g_send.at[low + n], g_recv.at[low + n], target
            )
            copy.start()
            copies.append(copy)
        started.extend(copies)
        return copies

    def sum_oo(stage, low, high):
        value = oo_send[stage]
        for index in range(low, high):
            value = value + oo_recv[index]
        return value

    axes1, axes2, axes3 = ("y", "x", "z"), ("x", "z", "y"), ("z", "y", "x")

    def take1(p, at, cols):
        return first(axes1[p], at, cols)

    def take2(p, at, cols):
        return keep1[:, at, :, cols] if p == 1 else keep1[at, :, :, cols]

    def take3(p, at, cols):
        return keep2[at, :, cols]

    round1 = []
    for d in (1, 2, 3, 0):
        g = (y + d) % 4
        rows = pl.ds(pl.multiple_of(g * 128, 128), 128)
        swap(g).wait_recv()
        acc[g, :, :, core] = acc[g, :, :, core] + recv0[rows, :].astype(F32).reshape(4, 4, 8, NV)
        if d:
            round1.append(deliver(0, send1, recv1, take1, BF16, 128, axes1, d, 0))
    round1.extend(exchange(0, send1, recv1, take1, BF16, 128, axes1, (1, 2)))
    lax.fori_loop(0, NV // 128, gram, 0)
    r = lax.broadcasted_iota(jnp.int32, (Q, Q), 0)
    c = lax.broadcasted_iota(jnp.int32, (Q, Q), 1)
    diagonal = jnp.where(r % 32 == c % 32, -gram_acc[...], 0.0)
    n = lax.broadcasted_iota(jnp.int32, (128, Q), 0)
    m = lax.broadcasted_iota(jnp.int32, (128, Q), 1)
    place = jnp.where(n == (orbital + m // 32) % 32, 1.0, 0.0).astype(F32)
    highest = lax.Precision.HIGHEST
    half = lax.dot_general(diagonal, place, NT, precision=highest, preferred_element_type=F32)
    half = jnp.sum(half.reshape(S, 32, 128), axis=1)
    n = lax.broadcasted_iota(jnp.int32, (32, 128), 0)
    placed = jnp.zeros((32, 128), F32)
    for s in range(S):
        placed = jnp.where(n == (orbital + s) % 32, half[s : s + 1, :], placed)
    oo_send[0] = placed

    for copy in round1:
        copy.wait_recv()
    for p, (start, width) in enumerate(PARTS):
        cols = pl.ds(start, width)
        keep1[:, :, :, cols] = total(p, take1, recv1, axes1[p], cols, (4, 4, 8, width))

    oo1 = oo_round(0, 0, [device((y + d) % 4, x, z, (core + e) % 2) for d in range(4) for e in range(2) if d or e])
    round2 = exchange(1, send2, recv2, take2, BF16, 32, axes2)
    for copy in round2:
        copy.wait_recv()
    for p, (start, width) in enumerate(PARTS):
        cols = pl.ds(start, width)
        keep2[:, :, cols] = total(p, take2, recv2, axes2[p], cols, (4, 8, width))

    round3 = exchange(2, send3, recv3, take3, F32, 8, axes3)
    for copy in oo1:
        copy.wait_recv()
    oo_send[1] = sum_oo(0, 0, 7)
    oo2 = oo_round(1, 7, [device(y, (x + d) % 4, (z + e) % 4, core) for d in range(4) for e in range(4) if d or e])
    for copy in round3:
        copy.wait_recv()
    for p, (start, width) in enumerate(PARTS):
        cols = pl.ds(start, width)
        vv_out[:, cols] = total(p, take3, recv3, axes3[p], cols, (8, width))
    for copy in oo2:
        copy.wait_recv()
    oo_out[...] = sum_oo(1, 7, 22)[:, :32]

    for at in (0, 1):
        gather(1, at).wait_send()
        gather(3, at).wait_send()
    pass_on().wait_send()

    @pl.when(core != h)
    def _():
        gather(0, 0).wait_send()
        gather(0, 1).wait_send()
        for ch in range(CH):
            swap_home(ch).wait_send()

    for ch in range(CH):
        shift_y(ch).wait_send()
        for l in (1, 2, 3):
            along_x(l, home, ch).wait_send()
    for l in (1, 2, 3):
        forward(2 * l + core, part.at[2 * l + core], l).wait_send()
    forward(1, home, 0).wait_send()

    def drain(s, _):
        for w in range(4):

            @pl.when(w != qz)
            def _():
                block_copy(s, w).wait_send()

        return 0

    lax.fori_loop(1, S, drain, 0)
    for copy in started:
        copy.wait_send()


def on_device(factors, occupied_energy, virtual_energy):
    dma = pltpu.SemaphoreType.DMA
    vmem = pl.BlockSpec(memory_space=pltpu.VMEM)
    return pl.pallas_call(
        kernel,
        out_shape=(
            jax.ShapeDtypeStruct((8, NV), F32),
            jax.ShapeDtypeStruct((32, 32), F32),
        ),
        in_specs=[pl.BlockSpec(memory_space=pl.ANY), pl.BlockSpec(memory_space=pltpu.SMEM), vmem],
        out_specs=(vmem, vmem),
        scratch_shapes=[
            pltpu.VMEM((NV, 128), F32),
            pltpu.VMEM((4, Q, NP), BF16),
            pltpu.VMEM((10, Q, NP), BF16),
            pltpu.VMEM((S, 4, Q, Q), BF16),
            pltpu.VMEM((S, NV, Q), BF16),
            pltpu.VMEM((S, NV, Q), BF16),
            pltpu.VMEM((4, 4, 4, 2, 8, NV), F32),
            pltpu.VMEM((Q, Q), F32),
            pltpu.VMEM((512, NV), BF16),
            pltpu.VMEM((512, NV), BF16),
            pltpu.VMEM((3, 128, NV), BF16),
            pltpu.VMEM((3, 128, NV), BF16),
            pltpu.VMEM((4, 4, 8, NV), F32),
            pltpu.VMEM((3, 32, NV), BF16),
            pltpu.VMEM((3, 32, NV), BF16),
            pltpu.VMEM((4, 8, NV), F32),
            pltpu.VMEM((3, 8, NV), F32),
            pltpu.VMEM((3, 8, NV), F32),
            pltpu.VMEM((2, 32, 128), F32),
            pltpu.VMEM((22, 32, 128), F32),
            dma((CH,)),
            dma((CH,)),
            dma((4, 2)),
            dma((4, 2)),
            dma((10, CH)),
            dma((CH,)),
            dma((4, CH)),
            dma((4,)),
            dma((S, 4)),
            dma((S, 4)),
            dma,
            dma((4,)),
            dma((4,)),
            dma((27,)),
            dma((27,)),
            dma((22,)),
            dma((22,)),
        ],
        compiler_params=pltpu.CompilerParams(
            collective_id=0, has_side_effects=True, vmem_limit_bytes=56 * 1024 * 1024
        ),
        cost_estimate=pl.CostEstimate(
            flops=14 * 10**9, bytes_accessed=2 * 10**6, transcendentals=0
        ),
    )(factors[0], occupied_energy, virtual_energy[None, :])


def solution(mesh):
    return jax.shard_map(
        on_device,
        mesh=mesh,
        in_specs=(P("occ", "vir", None), P(), P()),
        out_specs=(P(("occ", "vir"), None), P()),
        check_vma=False,
    )
```
